512 devices in a mesh: frames: 8 (over z_hi, y), pix: 64 (over x, z_lo, core).
Axes of the slice: x: 4, y: 4, z: 16 (z_hi: 2, z_lo: 8; z = z_hi * 8 + z_lo), core: 2. Of those that a mesh axis runs over, the one named last changes fastest.
Arguments:
- intensity: float32 [3072, 98304], P('frames', 'pix'), as said below
- circle_index: int32 [65536], P('pix'), may hold values from 0 to 1535
- pixel_mask: int32 [98304], P('pix'), may hold values 0 or 1
Outputs:
- correlation: float32 [5, 3072, 384], P(None, ('frames', 'pix'))
The draws below stay inside these ranges and needn't reach their ends.
Inputs may be any that keep to these rules, and one draw needn't show every extreme that they name: `circle_index`: each device's entries name columns of that device's own shard of the band. `intensity`: Positive.
All inputs are finite; a program needn't handle non-finite values. No bound on the sum of `pixel_mask` on one device may be relied on, other than what follows from the above.
Results may differ from the reference program's by a relative error of at most 0.0003.
Values sent between devices are 32-bit elements; how exact they have to be, the bound alone decides.
No kernel may reach another device: no remote copies, remote signals or barrier semaphores. Data moves between devices by JAX's collectives and lax.ppermute only.
A program may use at most 64 MiB of HBM per device.

```python
import math
import jax
import jax.numpy as jnp
from jax import lax

FB = 384
CIRCLE_DEV = 1024
BAND_DEV = 1536
FRAMES = 3072
CIRCLE = 65536
BAND = 98304
SHIFTS = 5
N_FRAMES = 8


def draw_intensity(key, part):
    key = jax.random.fold_in(key, 1)
    first_key = jax.random.fold_in(key, 0)
    second_key = jax.random.fold_in(key, 1)
    third_key = jax.random.fold_in(key, 2)
    fifth_key = jax.random.fold_in(key, 4)
    sixth_key = jax.random.fold_in(key, 5)
    frame_scale = jnp.exp(jax.random.uniform(first_key, (FRAMES, 1), jnp.float32) * math.log(10.0))
    position = jnp.arange(BAND, dtype=jnp.float32)[None, :] / BAND
    moment = jnp.arange(FRAMES, dtype=jnp.float32)[:, None] / FRAMES
    pixel_scale = jnp.exp(position * math.log(3.0)) * jnp.exp(jax.random.uniform(second_key, (1, BAND), jnp.float32) * math.log(10.0))
    elapsed = FRAMES * (1.6 * moment - 0.6 * moment * moment)
    rates = jnp.exp(jax.random.uniform(third_key, (4, 1, BAND), jnp.float32) * math.log(16.0 * N_FRAMES)) * (0.25 / FRAMES)
    amplitude = jnp.ones((4, 1, BAND), jnp.float32)
    floor_level = 0.05
    amplitude = amplitude / jnp.sqrt(amplitude[0] ** 2 + amplitude[1] ** 2 + amplitude[2] ** 2 + amplitude[3] ** 2)[None]
    offsets = jax.random.uniform(fifth_key, (4, 1, BAND), jnp.float32)
    real_part = jnp.zeros((FRAMES, BAND), jnp.float32)
    imag_part = jnp.zeros((FRAMES, BAND), jnp.float32)
    for mode in range(4):
        cycles = rates[mode] * elapsed + offsets[mode]
        cycles = cycles - jnp.floor(cycles)
        angle = cycles * (2.0 * math.pi)
        real_part = real_part + amplitude[mode] * jnp.cos(angle)
        imag_part = imag_part + amplitude[mode] * jnp.sin(angle)
    speckle = floor_level + real_part * real_part + imag_part * imag_part
    uniform_draw = jax.random.uniform(sixth_key, (FRAMES, BAND), jnp.float32)
    counting = 0.1 + 0.9 * -jnp.log1p(-uniform_draw)
    return (frame_scale * pixel_scale * speckle * counting).astype(jnp.float32)


def touch_ends(entries, stream_key, least, high):
    longest = entries.shape.index(max(entries.shape))
    spots = []
    for shift in (0, 1):
        where = [jax.random.randint(jax.random.fold_in(stream_key, axis), (), 0, length) for axis, length in enumerate(entries.shape)]
        where[longest] = (where[longest] + shift) % entries.shape[longest]
        spots.append(tuple(where))
    return entries.at[spots[0]].set(least).at[spots[1]].set(high)


def setup_inputs(seed: int = 0) -> dict:
    keys = jax.random.split(jax.random.key(seed), 4)
    return {
        "intensity": draw_intensity(jax.random.fold_in(keys[3], 71), 0),
        "circle_index": touch_ends(jax.random.randint(keys[1], (CIRCLE,), 0, BAND_DEV), jax.random.fold_in(keys[1], 1), 0, BAND_DEV - 1).astype(jnp.int32),
        "pixel_mask": touch_ends((jax.random.randint(keys[2], (BAND,), 0, 16) < 15).astype(jnp.int32), jax.random.fold_in(keys[2], 1), 0, 1),
    }


def cross_rows(left, right):
    return lax.dot_general(left, right, (((1,), (1,)), ((), ())), precision=lax.Precision.HIGHEST, preferred_element_type=jnp.float32)


def reference(intensity, circle_index, pixel_mask):
    owner_offset = (jnp.arange(CIRCLE, dtype=jnp.int32) // CIRCLE_DEV) * BAND_DEV
    columns = (circle_index + owner_offset).astype(jnp.int32)
    selected = jnp.take(intensity, columns, axis=1)
    weights = jnp.take(pixel_mask, columns).astype(jnp.float32)
    good_count = jnp.sum(weights)
    frame_sums = jnp.dot(selected, weights, precision=lax.Precision.HIGHEST)
    blocks = selected.reshape(N_FRAMES, FB, CIRCLE)
    block_sums = frame_sums.reshape(N_FRAMES, FB)

    def block_tiles(block_index):
        own_block = lax.dynamic_index_in_dim(blocks, block_index, 0, keepdims=False) * weights[None, :]
        own_sums = lax.dynamic_index_in_dim(block_sums, block_index, 0, keepdims=False)
        results = []
        for shift_step in range(SHIFTS):
            other_index = (block_index - shift_step) % N_FRAMES
            other_block = lax.dynamic_index_in_dim(blocks, other_index, 0, keepdims=False)
            other_sums = lax.dynamic_index_in_dim(block_sums, other_index, 0, keepdims=False)
            gram = cross_rows(own_block, other_block)
            results.append(gram * good_count / (own_sums[:, None] * other_sums[None, :]))
        return jnp.stack(results)

    tiles = lax.map(block_tiles, jnp.arange(N_FRAMES, dtype=jnp.int32))
    return jnp.transpose(tiles, (1, 0, 2, 3)).reshape(SHIFTS, FRAMES, FB)
```

```python
import functools

import jax
import jax.numpy as jnp
from jax import lax
from jax.experimental import pallas as pl
from jax.experimental.pallas import tpu as pltpu
from jax.sharding import PartitionSpec as P

NY, NX, NZL = 4, 4, 8
NZ = 2 * NZL
CLASSES = 4
SHIFTS = 5
ROWS = 6
WIDTHS = (256, 256)
VMEM = pl.BlockSpec(memory_space=pltpu.VMEM)
SMEM = pl.BlockSpec(memory_space=pltpu.SMEM)
PARAMS = pltpu.CompilerParams(vmem_limit_bytes=24 * 1024 * 1024)
F32 = jnp.float32


def device_id(x, y, z, core):
    return ((z // NZL) * NY + y) * (NX * NZL * 2) + (x * NZL + z % NZL) * 2 + core


def send(value, target):
    pairs = []
    for x in range(NX):
        for y in range(NY):
            for z in range(NZ):
                for core in range(2):
                    to = target(x, y, z, core)
                    if to is not None:
                        pairs.append((device_id(x, y, z, core), device_id(*to)))
    return lax.ppermute(value, ("frames", "pix"), pairs)


def split2(value):
    high = value.astype(jnp.bfloat16)
    return high, (value - high.astype(F32)).astype(jnp.bfloat16)


def split3(value):
    high = value.astype(jnp.bfloat16)
    return (high, *split2(value - high.astype(F32)))


def dot_nn(left, right):
    return jnp.dot(left, right, preferred_element_type=F32)


def dot_nt(left, right):
    return lax.dot_general(left, right, (((1,), (1,)), ((), ())), preferred_element_type=F32)


def select_kernel(begin, width, place, image, index, mask, first, second, count):
    band = image.shape[1]
    half = index.shape[1] // 2
    start = pl.multiple_of(place[0] * half, half)
    other = pl.multiple_of((1 - place[0]) * half, half)
    wanted = jnp.concatenate(
        [index[:, pl.ds(start + begin, width)], index[:, pl.ds(other + begin, width)]], axis=1
    )
    columns = lax.broadcasted_iota(jnp.int32, (band, 2 * width), 0)
    hot = (columns == wanted).astype(F32).astype(jnp.bfloat16)
    good = mask[...].astype(F32)
    picked = sum(dot_nn(part, hot) for part in reversed(split3(image[...] * good)))
    first[...] = picked[:, :width]
    second[...] = picked[:, width:]
    goods = dot_nn(jnp.broadcast_to(good, (8, band)).astype(jnp.bfloat16), hot)
    count[...] = jnp.broadcast_to(jnp.sum(goods, axis=1, keepdims=True), (8, 128))


def select(begin, width, place, image, index, mask):
    frames, band = image.shape
    block = jax.ShapeDtypeStruct((frames, width), F32)
    return pl.pallas_call(
        functools.partial(select_kernel, begin, width),
        out_shape=(block, block, jax.ShapeDtypeStruct((8, 128), F32)),
        in_specs=[SMEM, VMEM, VMEM, VMEM],
        out_specs=(VMEM, VMEM, VMEM),
        compiler_params=PARAMS,
        cost_estimate=pl.CostEstimate(
            flops=2 * frames * band * 2 * width * 3, bytes_accessed=frames * band * 4, transcendentals=0
        ),
        name="select",
    )(place, image, index, mask)


def gram_kernel(slots, has_previous, place, count, own, back1, back3, back2a, back2b, *refs):
    taken = 2 * len(slots) if has_previous else 0
    previous, outs, ordered = refs[:taken], refs[taken:-1], refs[-1]
    y, x, turn = place[1], place[2], place[3]
    frames, width = own.shape[1], own.shape[2]
    per_x = frames // NX
    per_class = per_x // CLASSES
    part = per_x // NZL
    one = jnp.ones((8, width), jnp.bfloat16)
    ones = jnp.concatenate([one, one, jnp.zeros_like(one)], axis=1)
    line = lax.broadcasted_iota(jnp.int32, (8, frames), 0)

    def from_back2(which):
        return jnp.where(which == 0, back2a[...], back2b[...])

    for at, slot in enumerate(slots):
        row_block = place[4] ^ slot
        for xc in range(NX):
            apart = x ^ xc
            chunk = jnp.where(apart == 3, 1, jnp.where(apart == 0, 0, apart + 1))
            for zl in range(NZL):
                kind = (zl - turn) & (CLASSES - 1)
                upper = zl // CLASSES
                ordered[chunk, kind, upper * part : (upper + 1) * part, :] = own[
                    row_block, xc * per_x + zl * part : xc * per_x + (zl + 1) * part, :
                ]
        high, low = split2(ordered[...].reshape(frames, width))
        rows = jnp.concatenate([jnp.concatenate([high, high, low], axis=1), ones], axis=0)
        flips = [row_block ^ (y < shift).astype(jnp.int32) for shift in range(SHIFTS)]
        others = (
            lambda: own[flips[0]],
            lambda: back1[flips[1]],
            lambda: from_back2(flips[2]),
            lambda: back3[flips[3]],
            lambda: own[1 - row_block],
        )
        sums = jnp.where(line == SHIFTS, 0.5 * count[0:1, 0:1], 0.0)
        outer, inner = outs[2 * at], outs[2 * at + 1]
        spots = []
        for side, (kept, given) in enumerate((((0, 1), (2, 3)), ((0, 2), (1, 3)))):
            for to, before, picks in (
                (inner, previous[2 * at + 1 : 2 * at + 2], kept),
                (outer, previous[2 * at : 2 * at + 1], given),
            ):
                for k, chunk in enumerate(picks):
                    for kind in range(2):
                        spots.append((to, before, (side, k, kind), chunk, side * 2 + kind))

        def store(spot, first, value):
            to, before, lead = spot[:3]
            where = (*lead, slice(first, first + value.shape[0]))
            to[where] = value + before[0][where] if before else value

        for shift, other in enumerate(others):
            high, low = split2(other())
            tile = dot_nt(rows, jnp.concatenate([high, low, high], axis=1))
            sums = jnp.where(line == shift, tile[frames:], sums)
            for spot in spots:
                begin = spot[3] * per_x + spot[4] * per_class
                store(spot, shift * per_class, tile[begin : begin + per_class])
        for spot in spots:
            store(spot, SHIFTS * per_class, sums)


def gram(slots, place, count, own, back1, back3, back2, previous=()):
    _, frames, width = own.shape
    operands = [place, count, own, back1, back3, *back2, *previous]
    lines = SHIFTS * frames // NX // CLASSES + 8
    result = jax.ShapeDtypeStruct((2, 2, 2, lines, frames), F32)
    return pl.pallas_call(
        functools.partial(gram_kernel, slots, bool(previous)),
        out_shape=(result,) * (2 * len(slots)),
        in_specs=[SMEM] + [VMEM] * (len(operands) - 1),
        out_specs=(VMEM,) * (2 * len(slots)),
        scratch_shapes=[pltpu.VMEM((NX, CLASSES, frames // NX // CLASSES, width), F32)],
        compiler_params=PARAMS,
        cost_estimate=pl.CostEstimate(
            flops=len(slots) * 5 * 2 * frames * frames * width * 3,
            bytes_accessed=8 * frames * width * 4 + len(slots) * 5 * frames * frames * 4,
            transcendentals=0,
        ),
        name="gram",
    )(*operands)


def share_kernel(place, near, up, down, far, out1, out2, out3, out4, local, parts):
    l2, core, wrong = place[5], place[6], place[7]
    total = (near[0] + up[...]) + (down[...] + far[...])
    for upper in range(2):
        for e in range(2):
            spot = (upper ^ l2, e ^ core)
            for shift in range(SHIFTS):
                begin = shift * 24 + upper * 12 + e * 6
                parts[(*spot, slice(shift * 6, shift * 6 + 6))] = total[begin : begin + 6]
            parts[(*spot, slice(32, 40))] = total[120:128]
            parts[(*spot, slice(30, 32))] = jnp.zeros((2, total.shape[1]), F32)
    right = wrong == 0
    out1[...] = jnp.where(right, parts[0, 1], parts[0, 0])
    out2[...] = jnp.where(right, parts[1, 1], parts[1, 0])
    out3[...] = jnp.where(right, parts[1, 0], parts[0, 1])
    out4[...] = parts[1, 1]
    local[...] = jnp.where(right, parts[0, 0], 0.0)


def share(place, near, up, down, far):
    frames = up.shape[-1]
    piece = jax.ShapeDtypeStruct((40, frames), F32)
    return pl.pallas_call(
        share_kernel,
        out_shape=(piece,) * 5,
        in_specs=[SMEM] + [VMEM] * 4,
        out_specs=(VMEM,) * 5,
        scratch_shapes=[pltpu.VMEM((2, 2, 40, frames), F32)],
        compiler_params=PARAMS,
        name="share",
    )(place, near, up, down, far)


def finish_kernel(place, local, first, second, third, fourth, out):
    total = (local[...] + first[...]) + (second[...] + third[...]) + fourth[...]
    frames = total.shape[1]
    sums = total[32 : 32 + SHIFTS]
    good = total[32 + SHIFTS : 33 + SHIFTS]
    line = lax.broadcasted_iota(jnp.int32, (ROWS, frames), 0)
    lane = lax.broadcasted_iota(jnp.int32, (ROWS, frames), 1)
    mine = jnp.where(lane == line + place[8], sums[0:1], 0.0)
    own = jnp.sum(mine, axis=1, keepdims=True)
    for shift in range(SHIFTS):
        tile = total[shift * ROWS : (shift + 1) * ROWS]
        out[shift] = tile * good / (own * sums[shift : shift + 1])


def finish(place, *pieces):
    frames = pieces[0].shape[1]
    return pl.pallas_call(
        finish_kernel,
        out_shape=jax.ShapeDtypeStruct((SHIFTS, ROWS, frames), F32),
        in_specs=[SMEM] + [VMEM] * 5,
        out_specs=VMEM,
        compiler_params=PARAMS,
        name="finish",
    )(place, *pieces)


def body(intensity, circle_index, pixel_mask):
    frame_at, pix_at = lax.axis_index("frames"), lax.axis_index("pix")
    zh, y = frame_at >> 2, frame_at & 3
    x, zl, core = pix_at >> 4, (pix_at >> 1) & 7, pix_at & 1
    first_label = ((zl >> 2) ^ zh) ^ 1
    own_row = first_label ^ core
    place = jnp.stack(
        [zh, y, x, zl & 3, own_row, zl >> 2, core, zh ^ core, pix_at * ROWS]
    ).astype(jnp.int32)
    index, mask = circle_index[None, :], pixel_mask[None, :]
    quarter = NZ // 4

    def up(value):
        return send(value, lambda x, y, z, c: (x, (y + 1) % NY, z, c))

    def down(value):
        return send(value, lambda x, y, z, c: (x, (y - 1) % NY, z, c))

    picked, begin = [], 0
    for width in WIDTHS:
        picked.append(select(begin, width, place, intensity, index, mask))
        begin += width
    met = []
    for first, second, _ in picked:
        if met:
            first, before = lax.optimization_barrier((first, met[-1][0]))
            second, also = lax.optimization_barrier((second, met[-1][1]))
            met[-1] = (before, also)
        met.append(
            (
                send(first, lambda x, y, z, c: (x, y, (z + quarter) % NZ, c)),
                send(second, lambda x, y, z, c: (x, y, (z - quarter) % NZ, c)),
            )
        )
    partial = ()
    for (_, _, count), arrived in zip(picked, met):
        own = jnp.stack(arrived)
        back1, back3 = up(own), down(own)
        back2 = (up(back1[0]), down(back3[1]))
        if not partial:
            partial = gram((1, 0), place, count, own, back1, back3, back2)
        else:
            give = gram((1,), place, count, own, back1, back3, back2, partial[:2])
            keep = gram((0,), place, count, own, back1, back3, back2, partial[2:])
            partial = (*give, *keep)

    def across(value):
        return send(value, lambda x, y, z, c: (x, y, z, 1 - c))

    def to_p(value):
        return send(value, lambda x, y, z, c: (x ^ 1, y, z, c))

    def to_q(value):
        return send(value, lambda x, y, z, c: (3 - x, y, z, c))

    give_outer, give_inner, keep_outer, keep_inner = partial
    other_outer = across(give_outer)
    other_inner = across(give_inner)
    outer = keep_outer + other_outer
    got = (to_p(outer[0]), to_q(outer[1]))
    inner = keep_inner + other_inner
    mine = [inner[0] + got[0], inner[1] + got[1]]
    near = mine[0][0] + to_q(mine[0][1])
    away = mine[1][0] + to_p(mine[1][1])
    from_below = send(near[1], lambda x, y, z, c: (x, y, (z + 1) % NZ, c))
    from_above = send(away[1], lambda x, y, z, c: (x, y, (z - 1) % NZ, c))
    from_two = send(away[0], lambda x, y, z, c: (x, y, (z + 2 - 4 * c) % NZ, c))
    pieces = share(place, near, from_below, from_above, from_two)

    def owner(right, wrong):
        def target(x, y, z, c):
            at_home = z // NZL == c
            hop = right if at_home else wrong
            if hop is None:
                return None
            upper, cross = hop
            to = (z ^ (4 * upper)) ^ (0 if at_home else NZL)
            return x, y, to, c ^ cross

        return target

    hops = (((0, 1), (0, 0)), ((1, 1), (1, 0)), ((1, 0), (0, 1)), (None, (1, 1)))
    moved = [send(piece, owner(*hop)) for piece, hop in zip(pieces, hops)]
    return finish(place, pieces[4], *moved)


def solution(mesh):
    return jax.shard_map(
        body,
        mesh=mesh,
        in_specs=(P("frames", "pix"), P("pix"), P("pix")),
        out_specs=P(None, ("frames", "pix"), None),
        check_vma=False,
    )
```

```python
import functools

import jax
import jax.numpy as jnp
from jax import lax
from jax.experimental import pallas as pl
from jax.experimental.pallas import tpu as pltpu
from jax.sharding import PartitionSpec as P

NY, NX, NZL = 4, 4, 8
NZ = 2 * NZL
CLASSES = 4
SHIFTS = 5
ROWS = 6
WIDTHS = (256, 256)
VMEM = pl.BlockSpec(memory_space=pltpu.VMEM)
SMEM = pl.BlockSpec(memory_space=pltpu.SMEM)
PARAMS = pltpu.CompilerParams(vmem_limit_bytes=24 * 1024 * 1024)
F32 = jnp.float32


def device_id(x, y, z, core):
    return ((z // NZL) * NY + y) * (NX * NZL * 2) + (x * NZL + z % NZL) * 2 + core


def send(value, target):
    pairs = []
    for x in range(NX):
        for y in range(NY):
            for z in range(NZ):
                for core in range(2):
                    to = target(x, y, z, core)
                    if to is not None:
                        pairs.append((device_id(x, y, z, core), device_id(*to)))
    return lax.ppermute(value, ("frames", "pix"), pairs)


def split2(value):
    high = value.astype(jnp.bfloat16)
    return high, (value - high.astype(F32)).astype(jnp.bfloat16)


def split3(value):
    high = value.astype(jnp.bfloat16)
    return (high, *split2(value - high.astype(F32)))


def dot_nn(left, right):
    return jnp.dot(left, right, preferred_element_type=F32)


def dot_nt(left, right):
    return lax.dot_general(left, right, (((1,), (1,)), ((), ())), preferred_element_type=F32)


def select_kernel(flip, place, image, index, mask, out, count):
    band = image.shape[1]
    half = index.shape[1] // 2
    begin = pl.multiple_of((place[0] ^ flip) * half, half)
    columns = lax.broadcasted_iota(jnp.int32, (band, half), 0)
    hot = (columns == index[:, pl.ds(begin, half)]).astype(F32).astype(jnp.bfloat16)
    good = mask[...].astype(F32)
    picked = sum(dot_nn(part, hot) for part in reversed(split3(image[...] * good)))
    out[...] = picked
    goods = dot_nn(jnp.broadcast_to(good, (8, band)).astype(jnp.bfloat16), hot)
    count[...] = jnp.broadcast_to(jnp.sum(goods, axis=1, keepdims=True), (8, 128))


def select(flip, place, image, index, mask):
    frames, band = image.shape
    half = index.shape[1] // 2
    block = jax.ShapeDtypeStruct((frames, half), F32)
    return pl.pallas_call(
        functools.partial(select_kernel, flip),
        out_shape=(block, jax.ShapeDtypeStruct((8, 128), F32)),
        in_specs=[SMEM, VMEM, VMEM, VMEM],
        out_specs=(VMEM, VMEM),
        compiler_params=PARAMS,
        cost_estimate=pl.CostEstimate(
            flops=2 * frames * band * half * 3, bytes_accessed=frames * band * 4, transcendentals=0
        ),
        name="select",
    )(place, image, index, mask)


def gram_kernel(slots, begin, has_previous, place, count, *refs):
    stay, move = refs[0:4], refs[4:8]
    taken = 2 * len(slots) if has_previous else 0
    previous, outs, ordered = refs[8 : 8 + taken], refs[8 + taken : -1], refs[-1]
    y, x, turn = place[1], place[2], place[3]
    frames, width = move[0].shape
    per_x = frames // NX
    per_class = per_x // CLASSES
    part = per_x // NZL
    one = jnp.ones((8, width), jnp.bfloat16)
    ones = jnp.concatenate([one, one, jnp.zeros_like(one)], axis=1)
    line = lax.broadcasted_iota(jnp.int32, (8, frames), 0)

    def block(back, which):
        return jnp.where(which == 0, stay[back][:, begin : begin + width], move[back][...])

    for at, slot in enumerate(slots):
        row_block = place[4] ^ slot
        left = block(0, row_block)
        for xc in range(NX):
            apart = x ^ xc
            chunk = jnp.where(apart == 3, 1, jnp.where(apart == 0, 0, apart + 1))
            for zl in range(NZL):
                kind = (zl - turn) & (CLASSES - 1)
                upper = zl // CLASSES
                ordered[chunk, kind, upper * part : (upper + 1) * part, :] = left[
                    xc * per_x + zl * part : xc * per_x + (zl + 1) * part, :
                ]
        high, low = split2(ordered[...].reshape(frames, width))
        rows = jnp.concatenate([jnp.concatenate([high, high, low], axis=1), ones], axis=0)
        sums = jnp.where(line == SHIFTS, count[0:1, 0:1], 0.0)
        if has_previous:
            sums = jnp.zeros_like(sums)
        outer, inner = outs[2 * at], outs[2 * at + 1]
        spots = []
        for side, (kept, given) in enumerate((((0, 1), (2, 3)), ((0, 2), (1, 3)))):
            for to, before, picks in (
                (inner, previous[2 * at + 1 : 2 * at + 2], kept),
                (outer, previous[2 * at : 2 * at + 1], given),
            ):
                for k, chunk in enumerate(picks):
                    for kind in range(2):
                        spots.append((to, before, (side, k, kind), chunk, side * 2 + kind))

        def store(spot, first, value):
            to, before, lead = spot[:3]
            where = (*lead, slice(first, first + value.shape[0]))
            to[where] = value + before[0][where] if before else value

        for shift in range(SHIFTS):
            if shift < 4:
                other = block(shift, row_block ^ (y < shift).astype(jnp.int32))
            else:
                other = block(0, 1 - row_block)
            high, low = split2(other)
            tile = dot_nt(rows, jnp.concatenate([high, low, high], axis=1))
            sums = jnp.where(line == shift, tile[frames:], sums)
            for spot in spots:
                first = spot[3] * per_x + spot[4] * per_class
                store(spot, shift * per_class, tile[first : first + per_class])
        for spot in spots:
            store(spot, SHIFTS * per_class, sums)


def gram(slots, begin, place, count, stay, move, previous=()):
    frames, width = move[0].shape
    operands = [place, count, *stay, *move, *previous]
    lines = SHIFTS * frames // NX // CLASSES + 8
    result = jax.ShapeDtypeStruct((2, 2, 2, lines, frames), F32)
    return pl.pallas_call(
        functools.partial(gram_kernel, slots, begin, bool(previous)),
        out_shape=(result,) * (2 * len(slots)),
        in_specs=[SMEM] + [VMEM] * (len(operands) - 1),
        out_specs=(VMEM,) * (2 * len(slots)),
        scratch_shapes=[pltpu.VMEM((NX, CLASSES, frames // NX // CLASSES, width), F32)],
        compiler_params=PARAMS,
        cost_estimate=pl.CostEstimate(
            flops=len(slots) * 5 * 2 * frames * frames * width * 3,
            bytes_accessed=8 * frames * width * 4 + len(slots) * 5 * frames * frames * 4,
            transcendentals=0,
        ),
        name="gram",
    )(*operands)


def share_kernel(place, near, up, down, far, out1, out2, out3, out4, local, parts):
    l2, core, wrong = place[5], place[6], place[7]
    total = (near[0] + up[...]) + (down[...] + far[...])
    for upper in range(2):
        for e in range(2):
            spot = (upper ^ l2, e ^ core)
            for shift in range(SHIFTS):
                begin = shift * 24 + upper * 12 + e * 6
                parts[(*spot, slice(shift * 6, shift * 6 + 6))] = total[begin : begin + 6]
            parts[(*spot, slice(32, 40))] = total[120:128]
            parts[(*spot, slice(30, 32))] = jnp.zeros((2, total.shape[1]), F32)
    right = wrong == 0
    out1[...] = jnp.where(right, parts[0, 1], parts[0, 0])
    out2[...] = jnp.where(right, parts[1, 1], parts[1, 0])
    out3[...] = jnp.where(right, parts[1, 0], parts[0, 1])
    out4[...] = parts[1, 1]
    local[...] = jnp.where(right, parts[0, 0], 0.0)


def share(place, near, up, down, far):
    frames = up.shape[-1]
    piece = jax.ShapeDtypeStruct((40, frames), F32)
    return pl.pallas_call(
        share_kernel,
        out_shape=(piece,) * 5,
        in_specs=[SMEM] + [VMEM] * 4,
        out_specs=(VMEM,) * 5,
        scratch_shapes=[pltpu.VMEM((2, 2, 40, frames), F32)],
        compiler_params=PARAMS,
        name="share",
    )(place, near, up, down, far)


def finish_kernel(place, local, first, second, third, fourth, out):
    total = (local[...] + first[...]) + (second[...] + third[...]) + fourth[...]
    frames = total.shape[1]
    sums = total[32 : 32 + SHIFTS]
    good = total[32 + SHIFTS : 33 + SHIFTS]
    line = lax.broadcasted_iota(jnp.int32, (ROWS, frames), 0)
    lane = lax.broadcasted_iota(jnp.int32, (ROWS, frames), 1)
    mine = jnp.where(lane == line + place[8], sums[0:1], 0.0)
    own = jnp.sum(mine, axis=1, keepdims=True)
    for shift in range(SHIFTS):
        tile = total[shift * ROWS : (shift + 1) * ROWS]
        out[shift] = tile * good / (own * sums[shift : shift + 1])


def finish(place, *pieces):
    frames = pieces[0].shape[1]
    return pl.pallas_call(
        finish_kernel,
        out_shape=jax.ShapeDtypeStruct((SHIFTS, ROWS, frames), F32),
        in_specs=[SMEM] + [VMEM] * 5,
        out_specs=VMEM,
        compiler_params=PARAMS,
        name="finish",
    )(place, *pieces)


def body(intensity, circle_index, pixel_mask):
    frame_at, pix_at = lax.axis_index("frames"), lax.axis_index("pix")
    zh, y = frame_at >> 2, frame_at & 3
    x, zl, core = pix_at >> 4, (pix_at >> 1) & 7, pix_at & 1
    place = jnp.stack(
        [zh, y, x, zl & 3, zh ^ core, zl >> 2, core, zh ^ core, pix_at * ROWS]
    ).astype(jnp.int32)
    index, mask = circle_index[None, :], pixel_mask[None, :]

    def after(value, *others):
        return lax.optimization_barrier((value, *others))[0]

    def around(value, *before):
        up = send(value, lambda x, y, z, c: (x, (y + 1) % NY, z, c))
        down = send(value, lambda x, y, z, c: (x, (y - 1) % NY, z, c))
        late = after(value, *before) if before else value
        opposite = send(late, lambda x, y, z, c: (x, (y + 2) % NY, z, c))
        return value, up, opposite, down

    given, _ = select(0, place, intensity, index, mask)
    moved = send(given, lambda x, y, z, c: (x, y, (z + NZL) % NZ, c))
    kept, count = select(1, place, intensity, after(index, given), mask)
    stay = around(kept)
    partial, begin = (), 0
    for width in WIDTHS:
        move = around(moved[:, begin : begin + width], *partial)
        if not partial:
            partial = gram((1, 0), begin, place, count, stay, move)
        else:
            give = gram((1,), begin, place, count, stay, move, partial[:2])
            keep = gram((0,), begin, place, count, stay, move, partial[2:])
            partial = (*give, *keep)
        begin += width

    def across(value):
        return send(value, lambda x, y, z, c: (x, y, z, 1 - c))

    def to_p(value):
        return send(value, lambda x, y, z, c: (x ^ 1, y, z, c))

    def to_q(value):
        return send(value, lambda x, y, z, c: (3 - x, y, z, c))

    give_outer, give_inner, keep_outer, keep_inner = partial
    other_outer = across(give_outer)
    other_inner = across(give_inner)
    outer = keep_outer + other_outer
    got = (to_p(outer[0]), to_q(outer[1]))
    inner = keep_inner + other_inner
    mine = [inner[0] + got[0], inner[1] + got[1]]
    near = mine[0][0] + to_q(mine[0][1])
    away = mine[1][0] + to_p(mine[1][1])
    from_below = send(near[1], lambda x, y, z, c: (x, y, (z + 1) % NZ, c))
    from_above = send(away[1], lambda x, y, z, c: (x, y, (z - 1) % NZ, c))
    from_two = send(away[0], lambda x, y, z, c: (x, y, (z + 2 - 4 * c) % NZ, c))
    pieces = share(place, near, from_below, from_above, from_two)

    def owner(right, wrong):
        def target(x, y, z, c):
            at_home = z // NZL == c
            hop = right if at_home else wrong
            if hop is None:
                return None
            upper, cross = hop
            to = (z ^ (4 * upper)) ^ (0 if at_home else NZL)
            return x, y, to, c ^ cross

        return target

    hops = (((0, 1), (0, 0)), ((1, 1), (1, 0)), ((1, 0), (0, 1)), (None, (1, 1)))
    moved = [send(piece, owner(*hop)) for piece, hop in zip(pieces, hops)]
    return finish(place, pieces[4], *moved)


def solution(mesh):
    return jax.shard_map(
        body,
        mesh=mesh,
        in_specs=(P("frames", "pix"), P("pix"), P("pix")),
        out_specs=P(None, ("frames", "pix"), None),
        check_vma=False,
    )
```

```python
import functools

import jax
import jax.numpy as jnp
from jax import lax
from jax.experimental import pallas as pl
from jax.experimental.pallas import tpu as pltpu
from jax.sharding import PartitionSpec as P

AXES = {"zh": 2, "y": 4, "x": 4, "l2": 2, "r": 4, "core": 2}
FRAMES, PIX = ("zh", "y"), ("x", "l2", "r", "core")
SHIFTS = 5
ROWS = 6
WIDTHS = (256, 256)
VMEM = pl.BlockSpec(memory_space=pltpu.VMEM)
SMEM = pl.BlockSpec(memory_space=pltpu.SMEM)
PARAMS = pltpu.CompilerParams(vmem_limit_bytes=24 * 1024 * 1024)
F32 = jnp.float32


def pass_on(value, axis, by):
    length = lax.axis_size(axis)
    return lax.ppermute(value, axis, [(i, (i + by) % length) for i in range(length)])


def split2(value):
    high = value.astype(jnp.bfloat16)
    return high, (value - high.astype(F32)).astype(jnp.bfloat16)


def split3(value):
    high = value.astype(jnp.bfloat16)
    return (high, *split2(value - high.astype(F32)))


def dot_nn(left, right):
    return jnp.dot(left, right, preferred_element_type=F32)


def dot_nt(left, right):
    return lax.dot_general(left, right, (((1,), (1,)), ((), ())), preferred_element_type=F32)


def select_kernel(flip, place, image, index, mask, out, count):
    band = image.shape[1]
    half = index.shape[1] // 2
    begin = pl.multiple_of((place[0] ^ flip) * half, half)
    columns = lax.broadcasted_iota(jnp.int32, (band, half), 0)
    hot = (columns == index[:, pl.ds(begin, half)]).astype(F32).astype(jnp.bfloat16)
    good = mask[...].astype(F32)
    picked = sum(dot_nn(part, hot) for part in reversed(split3(image[...] * good)))
    out[...] = picked
    goods = dot_nn(jnp.broadcast_to(good, (8, band)).astype(jnp.bfloat16), hot)
    count[...] = jnp.broadcast_to(jnp.sum(goods, axis=1, keepdims=True), (8, 128))


def select(flip, place, image, index, mask):
    frames, band = image.shape
    half = index.shape[1] // 2
    block = jax.ShapeDtypeStruct((frames, half), F32)
    return pl.pallas_call(
        functools.partial(select_kernel, flip),
        out_shape=(block, jax.ShapeDtypeStruct((8, 128), F32)),
        in_specs=[SMEM, VMEM, VMEM, VMEM],
        out_specs=(VMEM, VMEM),
        compiler_params=PARAMS,
        cost_estimate=pl.CostEstimate(
            flops=2 * frames * band * half * 3, bytes_accessed=frames * band * 4, transcendentals=0
        ),
        name="select",
    )(place, image, index, mask)


def gram_kernel(slots, begin, has_previous, place, count, *refs):
    stay, move = refs[0:4], refs[4:8]
    previous = refs[8 : 8 + len(slots)] if has_previous else ()
    outs, ordered = refs[8 + len(previous) : -1], refs[-1]
    zh, y, core = place[0], place[1], place[2]
    frames, width = move[0].shape
    owners = AXES["x"] * AXES["r"]
    mine = 2 * ROWS
    one = jnp.ones((8, width), jnp.bfloat16)
    ones = jnp.concatenate([one, one, jnp.zeros_like(one)], axis=1)
    line = lax.broadcasted_iota(jnp.int32, (16, frames), 0)

    def block(back, label):
        return jnp.where(label == zh, stay[back][:, begin : begin + width], move[back][...])

    for at, slot in enumerate(slots):
        first = (core ^ slot) == 0
        rows = []
        for label in range(2):
            left = block(0, label)
            for x in range(AXES["x"]):
                for r in range(AXES["r"]):
                    for l2 in range(2):
                        source = x * (frames // AXES["x"]) + (l2 * AXES["r"] + r) * mine
                        to = (x * AXES["r"] + r) * mine + l2 * ROWS
                        ordered[to : to + ROWS, :] = jnp.where(
                            first, left[source : source + ROWS], left[source + ROWS : source + mine]
                        )
            high, low = split2(ordered[...])
            rows.append(jnp.concatenate([high, high, low], axis=1))
        sums = jnp.zeros((16, frames), F32)
        if not has_previous:
            sums = jnp.where((line & 7) == SHIFTS, count[0:1, 0:1], sums)
        size = owners * mine
        for shift in range(SHIFTS):
            tiles = []
            for label in range(2):
                if shift < 4:
                    other = block(shift, label ^ (y < shift).astype(jnp.int32))
                else:
                    other = block(0, 1 - label)
                high, low = split2(other)
                tile = dot_nt(
                    jnp.concatenate([rows[label], ones], axis=0),
                    jnp.concatenate([high, low, high], axis=1),
                )
                sums = jnp.where(line == label * 8 + shift, tile[size : size + 1], sums)
                tiles.append(tile)
            for owner in range(owners):
                where = (owner // AXES["r"], owner % AXES["r"], slice(shift * 24, shift * 24 + 24))
                piece = jnp.concatenate(
                    [tile[owner * mine : (owner + 1) * mine] for tile in tiles], axis=0
                )
                outs[at][where] = piece + previous[at][where] if has_previous else piece
        for owner in range(owners):
            where = (owner // AXES["r"], owner % AXES["r"], slice(120, 136))
            outs[at][where] = sums + previous[at][where] if has_previous else sums


def gram(slots, begin, place, count, stay, move, previous=()):
    frames, width = move[0].shape
    operands = [place, count, *stay, *move, *previous]
    result = jax.ShapeDtypeStruct((AXES["x"], AXES["r"], 136, frames), F32)
    return pl.pallas_call(
        functools.partial(gram_kernel, slots, begin, bool(previous)),
        out_shape=(result,) * len(slots),
        in_specs=[SMEM] + [VMEM] * (len(operands) - 1),
        out_specs=(VMEM,) * len(slots),
        scratch_shapes=[pltpu.VMEM((frames // 2, width), F32)],
        compiler_params=PARAMS,
        cost_estimate=pl.CostEstimate(
            flops=len(slots) * 5 * 2 * frames * frames * width * 3,
            bytes_accessed=8 * frames * width * 4 + len(slots) * 5 * frames * frames * 4,
            transcendentals=0,
        ),
        name="gram",
    )(*operands)


def share_kernel(parts, out):
    total = (parts[0] + parts[1]) + (parts[2] + parts[3])
    for zh in range(2):
        for l2 in range(2):
            to = zh * 2 + l2
            for shift in range(SHIFTS):
                begin = shift * 24 + zh * 12 + l2 * ROWS
                out[to, shift * ROWS : (shift + 1) * ROWS] = total[begin : begin + ROWS]
            out[to, 30:32] = jnp.zeros((2, total.shape[1]), F32)
            out[to, 32:40] = total[120 + zh * 8 : 128 + zh * 8]


def share(parts):
    return pl.pallas_call(
        share_kernel,
        out_shape=jax.ShapeDtypeStruct((4, 40, parts.shape[-1]), F32),
        in_specs=[VMEM],
        out_specs=VMEM,
        compiler_params=PARAMS,
        name="share",
    )(parts)


def finish_kernel(place, parts, out):
    total = (parts[0] + parts[1]) + (parts[2] + parts[3])
    frames = total.shape[1]
    sums = total[32 : 32 + SHIFTS]
    good = total[32 + SHIFTS : 33 + SHIFTS]
    line = lax.broadcasted_iota(jnp.int32, (ROWS, frames), 0)
    lane = lax.broadcasted_iota(jnp.int32, (ROWS, frames), 1)
    mine = jnp.where(lane == line + place[3], sums[0:1], 0.0)
    own = jnp.sum(mine, axis=1, keepdims=True)
    for shift in range(SHIFTS):
        tile = total[shift * ROWS : (shift + 1) * ROWS]
        out[shift] = tile * good / (own * sums[shift : shift + 1])


def finish(place, parts):
    return pl.pallas_call(
        finish_kernel,
        out_shape=jax.ShapeDtypeStruct((SHIFTS, ROWS, parts.shape[-1]), F32),
        in_specs=[SMEM, VMEM],
        out_specs=VMEM,
        compiler_params=PARAMS,
        name="finish",
    )(place, parts)


def body(intensity, circle_index, pixel_mask):
    place = jnp.stack(
        [
            lax.axis_index("zh"),
            lax.axis_index("y"),
            lax.axis_index("core"),
            lax.axis_index(PIX) * ROWS,
        ]
    ).astype(jnp.int32)
    index, mask = circle_index[None, :], pixel_mask[None, :]

    def after(value, *others):
        return lax.optimization_barrier((value, *others))[0]

    def around(value):
        return value, pass_on(value, "y", 1), pass_on(value, "y", 2), pass_on(value, "y", -1)

    given, _ = select(0, place, intensity, index, mask)
    moved = pass_on(given, "zh", 1)
    kept, count = select(1, place, intensity, after(index, given), mask)
    stay = around(kept)
    partial, begin = (), 0
    for width in WIDTHS:
        move = around(moved[:, begin : begin + width])
        if not partial:
            partial = gram((1, 0), begin, place, count, stay, move)
        else:
            give = gram((1,), begin, place, count, stay, move, partial[:1])
            keep = gram((0,), begin, place, count, stay, move, partial[1:])
            partial = (*give, *keep)
        begin += width

    def exchange(parts, axis):
        return lax.all_to_all(parts, axis, 0, 0, tiled=True)

    give, keep = partial
    total = keep + pass_on(give, "core", 1)
    total = jnp.sum(exchange(total, "x"), axis=0)
    pieces = share(exchange(total, "r"))
    return finish(place, exchange(pieces, ("zh", "l2")))


def solution(mesh):
    split = jax.sharding.Mesh(mesh.devices.reshape(tuple(AXES.values())), tuple(AXES))
    return jax.shard_map(
        body,
        mesh=split,
        in_specs=(P(FRAMES, PIX), P(PIX), P(PIX)),
        out_specs=P(None, (*FRAMES, *PIX), None),
        check_vma=False,
    )
```

```python
import functools
import math

import jax
import jax.numpy as jnp
import numpy as np
from jax import lax
from jax.experimental import pallas as pl
from jax.experimental.pallas import tpu as pltpu
from jax.sharding import PartitionSpec as P

AXES = {"zh": 2, "y": 4, "x": 4, "l2": 2, "r": 4, "core": 2}
FRAMES, PIX = ("zh", "y"), ("x", "l2", "r", "core")
SHIFTS = 5
ROWS = 6
VMEM = pl.BlockSpec(memory_space=pltpu.VMEM)
SMEM = pl.BlockSpec(memory_space=pltpu.SMEM)
PARAMS = pltpu.CompilerParams(vmem_limit_bytes=24 * 1024 * 1024)
F32 = jnp.float32


def send(value, **moves):
    names = tuple(AXES)
    sizes = tuple(AXES.values())
    pairs = []
    for source in range(math.prod(sizes)):
        at = dict(zip(names, (int(i) for i in np.unravel_index(source, sizes))))
        to = [moves[name](at) % AXES[name] if name in moves else at[name] for name in names]
        pairs.append((source, int(np.ravel_multi_index(to, sizes))))
    return lax.ppermute(value, names, pairs)


def along_z(by):
    def target(at):
        z = at["zh"] * 8 + at["l2"] * 4 + at["r"]
        return (z + (by(at["core"]) if callable(by) else by)) % 16

    return {
        "zh": lambda at: target(at) // 8,
        "l2": lambda at: target(at) // 4,
        "r": lambda at: target(at),
    }


def split2(value):
    high = value.astype(jnp.bfloat16)
    return high, (value - high.astype(F32)).astype(jnp.bfloat16)


def split3(value):
    high = value.astype(jnp.bfloat16)
    return (high, *split2(value - high.astype(F32)))


def dot_nn(left, right):
    return jnp.dot(left, right, preferred_element_type=F32)


def dot_nt(left, right):
    return lax.dot_general(left, right, (((1,), (1,)), ((), ())), preferred_element_type=F32)


def select_kernel(flip, place, image, index, mask, out, count):
    band = image.shape[1]
    half = index.shape[1] // 2
    begin = pl.multiple_of((place[0] ^ flip) * half, half)
    columns = lax.broadcasted_iota(jnp.int32, (band, half), 0)
    hot = (columns == index[:, pl.ds(begin, half)]).astype(F32).astype(jnp.bfloat16)
    good = mask[...].astype(F32)
    picked = sum(dot_nn(part, hot) for part in reversed(split3(image[...] * good)))
    out[...] = picked
    goods = dot_nn(jnp.broadcast_to(good, (8, band)).astype(jnp.bfloat16), hot)
    count[...] = jnp.broadcast_to(jnp.sum(goods, axis=1, keepdims=True), (8, 128))


def select(flip, place, image, index, mask):
    frames, band = image.shape
    half = index.shape[1] // 2
    block = jax.ShapeDtypeStruct((frames, half), F32)
    return pl.pallas_call(
        functools.partial(select_kernel, flip),
        out_shape=(block, jax.ShapeDtypeStruct((8, 128), F32)),
        in_specs=[SMEM, VMEM, VMEM, VMEM],
        out_specs=(VMEM, VMEM),
        compiler_params=PARAMS,
        cost_estimate=pl.CostEstimate(
            flops=2 * frames * band * half * 3, bytes_accessed=frames * band * 4, transcendentals=0
        ),
        name="select",
    )(place, image, index, mask)


def gram_kernel(slots, shifts, place, count, stay0, move0, *refs):
    last = shifts == (2,)
    backs, refs = (refs[:3], refs[3:]) if last else (refs[:6], refs[6:])
    previous, outs, ordered = refs[: -1 - len(slots)], refs[-1 - len(slots) : -1], refs[-1]
    zh, y, core, x, r = (place[i] for i in (0, 1, 2, 4, 5))
    frames, width = move0.shape
    owners = AXES["x"] * AXES["r"]
    mine = 2 * ROWS
    one = jnp.ones((8, width), jnp.bfloat16)
    ones = jnp.concatenate([one, one, jnp.zeros_like(one)], axis=1)
    line = lax.broadcasted_iota(jnp.int32, (16, frames), 0)

    def block(back, label):
        if back == 0:
            stay, move = stay0[...], move0[...]
        else:
            at = 3 if back == 3 else 0
            stay, one, two = (ref[...] for ref in backs[at : at + 3])
            move = jnp.concatenate([one, two], axis=1)
        return jnp.where(label == zh, stay, move)

    def place_of(owner):
        apart = x ^ (owner // AXES["r"])
        turn = (owner % AXES["r"] - r) & 3
        side = turn >> 1
        near = jnp.where(side == 0, 2, 1)
        chunk = jnp.where(apart == 3, 3 - near, jnp.where(apart == 1, near, apart + (apart >> 1)))
        return side, chunk, turn & 1

    for at, slot in enumerate(slots):
        first = (core ^ slot) == 0
        out = outs[at]
        rows = []
        for label in range(2):
            left = block(0, label)
            for owner in range(owners):
                for l2 in range(2):
                    begin = owner // 4 * (frames // 4) + (l2 * 4 + owner % 4) * mine
                    to = owner * mine + l2 * ROWS
                    ordered[to : to + ROWS, :] = jnp.where(
                        first, left[begin : begin + ROWS], left[begin + ROWS : begin + mine]
                    )
            high, low = split2(ordered[...])
            rows.append(
                jnp.concatenate([jnp.concatenate([high, high, low], axis=1), ones], axis=0)
            )
        sums = jnp.where((line & 7) == SHIFTS, count[0:1, 0:1], 0.0)
        size = owners * mine
        if last:
            out[...] = previous[at][...]
        for shift in shifts:
            tiles = []
            for label in range(2):
                if shift < 4:
                    other = block(shift, label ^ (y < shift).astype(jnp.int32))
                else:
                    other = block(0, 1 - label)
                high, low = split2(other)
                tile = dot_nt(rows[label], jnp.concatenate([high, low, high], axis=1))
                sums = jnp.where(line == label * 8 + shift, tile[size : size + 1], sums)
                tiles.append(tile)
            for owner in range(owners):
                out[(*place_of(owner), slice(shift * 24, shift * 24 + 24))] = jnp.concatenate(
                    [tile[owner * mine : (owner + 1) * mine] for tile in tiles], axis=0
                )
        for owner in range(owners):
            where = (*place_of(owner), slice(120, 136))
            if last:
                out[where] = jnp.where((line & 7) == 2, sums, out[where])
            else:
                out[where] = sums


def gram(slots, shifts, place, count, stay0, move0, backs, previous=()):
    frames, width = move0.shape
    operands = [place, count, stay0, move0, *backs, *previous]
    result = jax.ShapeDtypeStruct((2, AXES["x"], 2, 136, frames), F32)
    return pl.pallas_call(
        functools.partial(gram_kernel, slots, shifts),
        out_shape=(result,) * len(slots),
        in_specs=[SMEM] + [VMEM] * (len(operands) - 1),
        out_specs=(VMEM,) * len(slots),
        scratch_shapes=[pltpu.VMEM((frames // 2, width), F32)],
        compiler_params=PARAMS,
        cost_estimate=pl.CostEstimate(
            flops=len(slots) * len(shifts) * 2 * frames * frames * width * 3,
            bytes_accessed=6 * frames * width * 4 + len(slots) * 5 * frames * frames * 4,
            transcendentals=0,
        ),
        name="gram",
    )(*operands)


def share_kernel(place, near, below, above, two, *outs):
    total = (near[0] + below[...]) + (above[...] + two[...])
    out = outs[-1]
    for zh in range(2):
        for l2 in range(2):
            to = (zh ^ place[0]) * 2 + (l2 ^ place[6])
            for shift in range(SHIFTS):
                begin = shift * 24 + zh * 12 + l2 * ROWS
                out[to, shift * ROWS : (shift + 1) * ROWS] = total[begin : begin + ROWS]
            out[to, 30:32] = jnp.zeros((2, total.shape[1]), F32)
            out[to, 32:40] = total[120 + zh * 8 : 128 + zh * 8]
    for to in range(4):
        outs[to][...] = out[to]


def share(place, *parts):
    frames = parts[-1].shape[-1]
    return pl.pallas_call(
        share_kernel,
        out_shape=(jax.ShapeDtypeStruct((40, frames), F32),) * 4,
        in_specs=[SMEM] + [VMEM] * 4,
        out_specs=(VMEM,) * 4,
        scratch_shapes=[pltpu.VMEM((4, 40, frames), F32)],
        compiler_params=PARAMS,
        name="share",
    )(place, *parts)


def finish_kernel(place, one, two, three, four, out):
    total = (one[...] + two[...]) + (three[...] + four[...])
    frames = total.shape[1]
    sums = total[32 : 32 + SHIFTS]
    good = total[32 + SHIFTS : 33 + SHIFTS]
    line = lax.broadcasted_iota(jnp.int32, (ROWS, frames), 0)
    lane = lax.broadcasted_iota(jnp.int32, (ROWS, frames), 1)
    mine = jnp.where(lane == line + place[3], sums[0:1], 0.0)
    own = jnp.sum(mine, axis=1, keepdims=True)
    for shift in range(SHIFTS):
        tile = total[shift * ROWS : (shift + 1) * ROWS]
        out[shift] = tile * good / (own * sums[shift : shift + 1])


def finish(place, *parts):
    return pl.pallas_call(
        finish_kernel,
        out_shape=jax.ShapeDtypeStruct((SHIFTS, ROWS, parts[0].shape[-1]), F32),
        in_specs=[SMEM] + [VMEM] * 4,
        out_specs=VMEM,
        compiler_params=PARAMS,
        name="finish",
    )(place, *parts)


def body(intensity, circle_index, pixel_mask):
    place = jnp.stack(
        [
            lax.axis_index("zh"),
            lax.axis_index("y"),
            lax.axis_index("core"),
            lax.axis_index(PIX) * ROWS,
            lax.axis_index("x"),
            lax.axis_index("r"),
            lax.axis_index("l2"),
        ]
    ).astype(jnp.int32)
    index, mask = circle_index[None, :], pixel_mask[None, :]

    def after(value, *others):
        return lax.optimization_barrier((value, *others))[0]

    def up(value):
        return send(value, y=lambda at: at["y"] + 1)

    def down(value):
        return send(value, y=lambda at: at["y"] - 1)

    given, _ = select(0, place, intensity, index, mask)
    moved = send(given, zh=lambda at: at["zh"] + 1)
    kept, count = select(1, place, intensity, after(index, given), mask)
    kept1, kept3 = up(kept), down(kept)
    kept2 = send(kept, y=lambda at: at["y"] + 2)
    half = moved.shape[1] // 2
    one, two, *_ = lax.optimization_barrier(
        (moved[:, :half], moved[:, half:], kept1, kept2, kept3)
    )
    one1, two3 = up(one), down(two)
    two1, one3 = up(two), down(one)
    moved2 = (up(one1), down(two3))
    backs = (kept1, one1, two1, kept3, one3, two3)
    early = gram((1, 0), (0, 1, 3, 4), place, count, kept, moved, backs)
    (give,) = gram((1,), (2,), place, count, kept, moved, (kept2, *moved2), early[:1])
    (keep,) = gram((0,), (2,), place, count, kept, moved, (kept2, *moved2), early[1:])

    def to_p(value):
        return send(value, x=lambda at: at["x"] ^ 1)

    def to_q(value):
        return send(value, x=lambda at: 3 - at["x"])

    total = keep + send(give, core=lambda at: 1 - at["core"])
    near = total[0, :2] + to_p(total[0, 2:])
    away = total[1, :2] + to_q(total[1, 2:])
    near = near[0] + to_q(near[1])
    away = away[0] + to_p(away[1])
    below = send(near[1], **along_z(1))
    above = send(away[1], **along_z(-1))
    middle = send(away[0], **along_z(lambda core: 2 - 4 * core))
    pieces = share(place, near, below, above, middle)
    far = send(pieces[2], zh=lambda at: at["zh"] + 1)
    farther = send(pieces[3], zh=lambda at: at["zh"] + 1, l2=lambda at: at["l2"] + 1)
    next_one = send(pieces[1], l2=lambda at: at["l2"] + 1)
    return finish(place, pieces[0], far, farther, next_one)


def solution(mesh):
    split = jax.sharding.Mesh(mesh.devices.reshape(tuple(AXES.values())), tuple(AXES))
    return jax.shard_map(
        body,
        mesh=split,
        in_specs=(P(FRAMES, PIX), P(PIX), P(PIX)),
        out_specs=P(None, (*FRAMES, *PIX), None),
        check_vma=False,
    )
```

```python
import functools
import math

import jax
import jax.numpy as jnp
import numpy as np
from jax import lax
from jax.experimental import pallas as pl
from jax.experimental.pallas import tpu as pltpu
from jax.sharding import PartitionSpec as P

AXES = {"zh": 2, "y": 4, "x": 4, "l2": 2, "r": 4, "core": 2}
FRAMES, PIX = ("zh", "y"), ("x", "l2", "r", "core")
SHIFTS = 5
ROWS = 6
ROOM = 384
VMEM = pl.BlockSpec(memory_space=pltpu.VMEM)
SMEM = pl.BlockSpec(memory_space=pltpu.SMEM)
PARAMS = pltpu.CompilerParams(vmem_limit_bytes=24 * 1024 * 1024)
F32 = jnp.float32


def send(value, **moves):
    names = tuple(AXES)
    sizes = tuple(AXES.values())
    pairs = []
    for source in range(math.prod(sizes)):
        at = dict(zip(names, (int(i) for i in np.unravel_index(source, sizes))))
        to = [moves[name](at) % AXES[name] if name in moves else at[name] for name in names]
        pairs.append((source, int(np.ravel_multi_index(to, sizes))))
    return lax.ppermute(value, names, pairs)


def along_z(by):
    def target(at):
        z = at["zh"] * 8 + at["l2"] * 4 + at["r"]
        return (z + (by(at["core"]) if callable(by) else by)) % 16

    return {
        "zh": lambda at: target(at) // 8,
        "l2": lambda at: target(at) // 4,
        "r": lambda at: target(at),
    }


def split2(value):
    high = value.astype(jnp.bfloat16)
    return high, (value - high.astype(F32)).astype(jnp.bfloat16)


def split3(value):
    high = value.astype(jnp.bfloat16)
    return (high, *split2(value - high.astype(F32)))


def as_bf16(value):
    return value.astype(F32).astype(jnp.bfloat16)


def spread(row, lines):
    return jnp.broadcast_to(row, (lines, row.shape[1]))


def dot_nn(left, right):
    return jnp.dot(left, right, preferred_element_type=F32)


def dot_nt(left, right):
    return lax.dot_general(left, right, (((1,), (1,)), ((), ())), preferred_element_type=F32)


def chosen(index, mask, begin, size):
    lanes = 128
    groups = mask.shape[1] // lanes
    padded = -(-groups // 16) * 16
    upper = lax.broadcasted_iota(jnp.int32, (padded, index.shape[1]), 0) == (index >> 7)
    lower = lax.broadcasted_iota(jnp.int32, (lanes, index.shape[1]), 0) == (index & (lanes - 1))
    times = dot_nt(as_bf16(upper), as_bf16(lower))
    rows = [mask[:, i * lanes : (i + 1) * lanes] for i in range(groups)]
    rows.append(jnp.zeros((padded - groups, lanes), jnp.int32))
    times = times * jnp.concatenate(rows, axis=0).astype(F32)
    used = as_bf16(times > 0)
    ahead = lax.broadcasted_iota(jnp.int32, (lanes, lanes), 0) < lax.broadcasted_iota(
        jnp.int32, (lanes, lanes), 1
    )
    above = lax.broadcasted_iota(jnp.int32, (padded, padded), 1) < lax.broadcasted_iota(
        jnp.int32, (padded, padded), 0
    )
    before = jnp.sum(dot_nn(as_bf16(above), used), axis=1, keepdims=True)
    number = dot_nn(used, as_bf16(ahead)) + before
    number = jnp.where(times > 0, number, -1.0).astype(jnp.int32)

    def in_line(value):
        return jnp.concatenate([value[i : i + 1] for i in range(groups)], axis=1)

    wanted = lax.broadcasted_iota(jnp.int32, (size, mask.shape[1]), 0) + begin
    total = jnp.sum(jnp.sum(used.astype(F32), axis=1, keepdims=True), axis=0, keepdims=True)
    return as_bf16(wanted == in_line(number)), in_line(times), total


def select_kernel(compact, flip, place, image, index, mask, out, weights, info):
    band = image.shape[1]
    size = out.shape[1]
    begin = (place[0] ^ flip) * size
    if compact:
        hot, times, total = chosen(index[...], mask[...], begin, size)
        picked = sum(dot_nt(part, hot) for part in reversed(split3(image[...])))
        weight = sum(dot_nt(part, hot) for part in reversed(split2(spread(times, 16))))
        over = jnp.where(total > 2.0 * size, 1.0, 0.0)
    else:
        columns = lax.broadcasted_iota(jnp.int32, (band, size), 0)
        hot = as_bf16(columns == index[:, pl.ds(pl.multiple_of(begin, size), size)])
        picked = sum(dot_nn(part, hot) for part in reversed(split3(image[...])))
        weight = dot_nn(spread(mask[...].astype(F32), 16).astype(jnp.bfloat16), hot)
        over = jnp.zeros((1, 1), F32)
    out[...] = picked
    weights[...] = weight
    count = jnp.sum(weight[0:1], axis=1, keepdims=True)
    line = lax.broadcasted_iota(jnp.int32, (8, 128), 0)
    info[...] = jnp.where(line == 0, count, over)


def select(compact, flip, place, image, index, mask):
    frames, band = image.shape
    size = ROOM if compact else index.shape[1] // 2
    return pl.pallas_call(
        functools.partial(select_kernel, compact, flip),
        out_shape=(
            jax.ShapeDtypeStruct((frames, size), F32),
            jax.ShapeDtypeStruct((16, size), F32),
            jax.ShapeDtypeStruct((8, 128), F32),
        ),
        in_specs=[SMEM, VMEM, VMEM, VMEM],
        out_specs=(VMEM, VMEM, VMEM),
        compiler_params=PARAMS,
        cost_estimate=pl.CostEstimate(
            flops=2 * frames * band * size * 3, bytes_accessed=frames * band * 4, transcendentals=0
        ),
        name="select",
    )(place, image, index, mask)


def gram_kernel(slots, shifts, place, info, weights, stay0, move0, *refs):
    last = shifts == (2,)
    backs, refs = (refs[:3], refs[3:]) if last else (refs[:6], refs[6:])
    previous, refs = refs[: -2 - len(slots)], refs[-2 - len(slots) :]
    outs, ordered, rows = refs[: len(slots)], refs[-2], refs[-1]
    zh, y, core, x, r = (place[i] for i in (0, 1, 2, 4, 5))
    frames, width = move0.shape
    owners = AXES["x"] * AXES["r"]
    mine = 2 * ROWS
    share_of = owners * mine
    size = len(slots) * share_of
    line = lax.broadcasted_iota(jnp.int32, (16, frames), 0)

    def terms(value):
        high, low = split2(value)
        return jnp.concatenate([high, low, high], axis=1)

    def blocks(back):
        if back == 0:
            return terms(stay0[...]), terms(move0[...])
        stay, one, two = backs[3:] if back == 3 else backs[:3]
        return terms(stay[...]), terms(jnp.concatenate([one[...], two[...]], axis=1))

    def place_of(owner):
        apart = x ^ (owner // AXES["r"])
        turn = (owner % AXES["r"] - r) & 3
        side = turn >> 1
        near = jnp.where(side == 0, 2, 1)
        chunk = jnp.where(apart == 3, 3 - near, jnp.where(apart == 1, near, apart + (apart >> 1)))
        return side, chunk, turn & 1

    for kind, left in enumerate((stay0[...], move0[...])):
        for at, slot in enumerate(slots):
            first = (core ^ slot) == 0
            for owner in range(owners):
                for l2 in range(2):
                    begin = owner // 4 * (frames // 4) + (l2 * 4 + owner % 4) * mine
                    to = at * share_of + owner * mine + l2 * ROWS
                    ordered[to : to + ROWS, :] = jnp.where(
                        first, left[begin : begin + ROWS], left[begin + ROWS : begin + mine]
                    )
        for begin, value in ((0, ordered[...] * weights[0:1]), (size, weights[...])):
            high, low = split2(value)
            rows[kind, begin : begin + value.shape[0], :] = jnp.concatenate(
                [high, high, low], axis=1
            )
    sums = jnp.where((line & 7) == SHIFTS, info[0:1, 0:1], 0.0)
    sums = jnp.where((line & 7) == SHIFTS + 1, info[1:2, 0:1], sums)
    if last:
        for out, before in zip(outs, previous):
            out[...] = before[...]
    here = None if last else blocks(0)
    for shift in shifts:
        if shift == 4:
            flip, right = 1, here
        else:
            flip = (y < shift).astype(jnp.int32)
            right = here if shift == 0 else blocks(shift)
        stay, move = (dot_nt(rows[kind ^ flip], right[kind]) for kind in range(2))
        swap = (zh ^ flip) == 1
        tiles = jnp.where(swap, move, stay), jnp.where(swap, stay, move)
        for label in range(2):
            sums = jnp.where(line == label * 8 + shift, tiles[label][size : size + 1], sums)
        for at, out in enumerate(outs):
            for owner in range(owners):
                begin = at * share_of + owner * mine
                out[(*place_of(owner), slice(shift * 24, shift * 24 + 24))] = jnp.concatenate(
                    [tile[begin : begin + mine] for tile in tiles], axis=0
                )
    for out in outs:
        for owner in range(owners):
            where = (*place_of(owner), slice(120, 136))
            out[where] = jnp.where((line & 7) == 2, sums, out[where]) if last else sums


def gram(slots, shifts, place, info, weights, stay0, move0, backs, previous=()):
    frames, width = move0.shape
    operands = [place, info, weights, stay0, move0, *backs, *previous]
    result = jax.ShapeDtypeStruct((2, AXES["x"], 2, 136, frames), F32)
    lines = len(slots) * frames // 2
    return pl.pallas_call(
        functools.partial(gram_kernel, slots, shifts),
        out_shape=(result,) * len(slots),
        in_specs=[SMEM] + [VMEM] * (len(operands) - 1),
        out_specs=(VMEM,) * len(slots),
        scratch_shapes=[
            pltpu.VMEM((lines, width), F32),
            pltpu.VMEM((2, lines + 16, 3 * width), jnp.bfloat16),
        ],
        compiler_params=PARAMS,
        cost_estimate=pl.CostEstimate(
            flops=len(slots) * len(shifts) * 2 * frames * frames * width * 3,
            bytes_accessed=6 * frames * width * 4 + len(slots) * 5 * frames * frames * 4,
            transcendentals=0,
        ),
        name="gram",
    )(*operands)


def share_kernel(place, near, below, above, two, *outs):
    total = (near[0] + below[...]) + (above[...] + two[...])
    out = outs[-1]
    for zh in range(2):
        for l2 in range(2):
            to = (zh ^ place[0]) * 2 + (l2 ^ place[6])
            for shift in range(SHIFTS):
                begin = shift * 24 + zh * 12 + l2 * ROWS
                out[to, shift * ROWS : (shift + 1) * ROWS] = total[begin : begin + ROWS]
            out[to, 30:32] = jnp.zeros((2, total.shape[1]), F32)
            out[to, 32:40] = total[120 + zh * 8 : 128 + zh * 8]
    for to in range(4):
        outs[to][...] = out[to]


def share(place, *parts):
    frames = parts[-1].shape[-1]
    return pl.pallas_call(
        share_kernel,
        out_shape=(jax.ShapeDtypeStruct((40, frames), F32),) * 4,
        in_specs=[SMEM] + [VMEM] * 4,
        out_specs=(VMEM,) * 4,
        scratch_shapes=[pltpu.VMEM((4, 40, frames), F32)],
        compiler_params=PARAMS,
        name="share",
    )(place, *parts)


def finish_kernel(place, one, two, three, four, out, missing):
    total = (one[...] + two[...]) + (three[...] + four[...])
    frames = total.shape[1]
    sums = total[32 : 32 + SHIFTS]
    good = total[32 + SHIFTS : 33 + SHIFTS]
    line = lax.broadcasted_iota(jnp.int32, (ROWS, frames), 0)
    lane = lax.broadcasted_iota(jnp.int32, (ROWS, frames), 1)
    mine = jnp.where(lane == line + place[3], sums[0:1], 0.0)
    own = jnp.sum(mine, axis=1, keepdims=True)
    for shift in range(SHIFTS):
        tile = total[shift * ROWS : (shift + 1) * ROWS]
        out[shift] = tile * good / (own * sums[shift : shift + 1])
    missing[...] = jnp.broadcast_to(total[33 + SHIFTS : 34 + SHIFTS, :128], (8, 128))


def finish(place, *parts):
    return pl.pallas_call(
        finish_kernel,
        out_shape=(
            jax.ShapeDtypeStruct((SHIFTS, ROWS, parts[0].shape[-1]), F32),
            jax.ShapeDtypeStruct((8, 128), F32),
        ),
        in_specs=[SMEM] + [VMEM] * 4,
        out_specs=(VMEM, VMEM),
        compiler_params=PARAMS,
        name="finish",
    )(place, *parts)


def correlate(compact, place, intensity, index, mask):
    def after(value, *others):
        return lax.optimization_barrier((value, *others))[0]

    def up(value):
        return send(value, y=lambda at: at["y"] + 1)

    def down(value):
        return send(value, y=lambda at: at["y"] - 1)

    given, *_ = select(compact, 0, place, intensity, index, mask)
    moved = send(given, zh=lambda at: at["zh"] + 1)
    kept, weights, info = select(compact, 1, place, intensity, after(index, given), mask)
    kept1, kept3 = up(kept), down(kept)
    kept2 = send(kept, y=lambda at: at["y"] + 2)
    half = 256
    one, two, *_ = lax.optimization_barrier(
        (moved[:, :half], moved[:, half:], kept1, kept2, kept3)
    )
    one1, two3 = up(one), down(two)
    two1, one3 = up(two), down(one)
    moved2 = (up(one1), down(two3))
    backs = (kept1, one1, two1, kept3, one3, two3)
    early = gram((1, 0), (0, 1, 3, 4), place, info, weights, kept, moved, backs)
    (give,) = gram((1,), (2,), place, info, weights, kept, moved, (kept2, *moved2), early[:1])
    (keep,) = gram((0,), (2,), place, info, weights, kept, moved, (kept2, *moved2), early[1:])

    def to_p(value):
        return send(value, x=lambda at: at["x"] ^ 1)

    def to_q(value):
        return send(value, x=lambda at: 3 - at["x"])

    total = keep + send(give, core=lambda at: 1 - at["core"])
    near = total[0, :2] + to_p(total[0, 2:])
    away = total[1, :2] + to_q(total[1, 2:])
    near = near[0] + to_q(near[1])
    away = away[0] + to_p(away[1])
    below = send(near[1], **along_z(1))
    above = send(away[1], **along_z(-1))
    middle = send(away[0], **along_z(lambda core: 2 - 4 * core))
    pieces = share(place, near, below, above, middle)
    far = send(pieces[2], zh=lambda at: at["zh"] + 1)
    farther = send(pieces[3], zh=lambda at: at["zh"] + 1, l2=lambda at: at["l2"] + 1)
    next_one = send(pieces[1], l2=lambda at: at["l2"] + 1)
    return finish(place, pieces[0], far, farther, next_one)


def body(intensity, circle_index, pixel_mask):
    place = jnp.stack(
        [
            lax.axis_index("zh"),
            lax.axis_index("y"),
            lax.axis_index("core"),
            lax.axis_index(PIX) * ROWS,
            lax.axis_index("x"),
            lax.axis_index("r"),
            lax.axis_index("l2"),
        ]
    ).astype(jnp.int32)
    operands = (place, intensity, circle_index[None, :], pixel_mask[None, :])
    result, missing = correlate(True, *operands)
    return lax.cond(
        missing[0, 0] > 0.5,
        lambda result, *operands: correlate(False, *operands)[0],
        lambda result, *operands: result,
        result,
        *operands,
    )


def solution(mesh):
    split = jax.sharding.Mesh(mesh.devices.reshape(tuple(AXES.values())), tuple(AXES))
    return jax.shard_map(
        body,
        mesh=split,
        in_specs=(P(FRAMES, PIX), P(PIX), P(PIX)),
        out_specs=P(None, (*FRAMES, *PIX), None),
        check_vma=False,
    )
```

```python
import functools
import math

import jax
import jax.numpy as jnp
import numpy as np
from jax import lax
from jax.experimental import pallas as pl
from jax.experimental.pallas import tpu as pltpu
from jax.sharding import PartitionSpec as P

AXES = {"zh": 2, "y": 4, "x": 4, "l2": 2, "r": 4, "core": 2}
FRAMES, PIX = ("zh", "y"), ("x", "l2", "r", "core")
SHIFTS = 5
ROWS = 6
ROOM = 384
VMEM = pl.BlockSpec(memory_space=pltpu.VMEM)
SMEM = pl.BlockSpec(memory_space=pltpu.SMEM)
PARAMS = pltpu.CompilerParams(vmem_limit_bytes=24 * 1024 * 1024)
F32 = jnp.float32


def send(value, **moves):
    names = tuple(AXES)
    sizes = tuple(AXES.values())
    pairs = []
    for source in range(math.prod(sizes)):
        at = dict(zip(names, (int(i) for i in np.unravel_index(source, sizes))))
        to = [moves[name](at) % AXES[name] if name in moves else at[name] for name in names]
        pairs.append((source, int(np.ravel_multi_index(to, sizes))))
    return lax.ppermute(value, names, pairs)


def along_z(by):
    def target(at):
        z = at["zh"] * 8 + at["l2"] * 4 + at["r"]
        return (z + (by(at["core"]) if callable(by) else by)) % 16

    return {
        "zh": lambda at: target(at) // 8,
        "l2": lambda at: target(at) // 4,
        "r": lambda at: target(at),
    }


def split2(value):
    high = value.astype(jnp.bfloat16)
    return high, (value - high.astype(F32)).astype(jnp.bfloat16)


def split3(value):
    high = value.astype(jnp.bfloat16)
    return (high, *split2(value - high.astype(F32)))


def as_bf16(value):
    return value.astype(F32).astype(jnp.bfloat16)


def spread(row, lines):
    return jnp.broadcast_to(row, (lines, row.shape[1]))


def dot_nn(left, right):
    return jnp.dot(left, right, preferred_element_type=F32)


def dot_nt(left, right):
    return lax.dot_general(left, right, (((1,), (1,)), ((), ())), preferred_element_type=F32)


def chosen(index, mask, begin, size):
    lanes = 128
    groups = mask.shape[1] // lanes
    padded = -(-groups // 16) * 16
    upper = lax.broadcasted_iota(jnp.int32, (padded, index.shape[1]), 0) == (index >> 7)
    lower = lax.broadcasted_iota(jnp.int32, (lanes, index.shape[1]), 0) == (index & (lanes - 1))
    times = dot_nt(as_bf16(upper), as_bf16(lower))
    rows = [mask[:, i * lanes : (i + 1) * lanes] for i in range(groups)]
    rows.append(jnp.zeros((padded - groups, lanes), jnp.int32))
    times = times * jnp.concatenate(rows, axis=0).astype(F32)
    used = as_bf16(times > 0)
    ahead = lax.broadcasted_iota(jnp.int32, (lanes, lanes), 0) < lax.broadcasted_iota(
        jnp.int32, (lanes, lanes), 1
    )
    above = lax.broadcasted_iota(jnp.int32, (padded, padded), 1) < lax.broadcasted_iota(
        jnp.int32, (padded, padded), 0
    )
    before = jnp.sum(dot_nn(as_bf16(above), used), axis=1, keepdims=True)
    number = dot_nn(used, as_bf16(ahead)) + before
    number = jnp.where(times > 0, number, -1.0).astype(jnp.int32)

    def in_line(value):
        return jnp.concatenate([value[i : i + 1] for i in range(groups)], axis=1)

    wanted = lax.broadcasted_iota(jnp.int32, (size, mask.shape[1]), 0) + begin
    total = jnp.sum(jnp.sum(used.astype(F32), axis=1, keepdims=True), axis=0, keepdims=True)
    return as_bf16(wanted == in_line(number)), in_line(times), total


def select_kernel(compact, flip, place, image, index, mask, out, weights, info):
    band = image.shape[1]
    size = out.shape[1]
    begin = (place[0] ^ flip) * size
    if compact:
        hot, times, total = chosen(index[...], mask[...], begin, size)
        picked = sum(dot_nt(part, hot) for part in reversed(split3(image[...])))
        weight = sum(dot_nt(part, hot) for part in reversed(split2(spread(times, 16))))
        over = jnp.where(total > 2.0 * size, 1.0, 0.0)
    else:
        columns = lax.broadcasted_iota(jnp.int32, (band, size), 0)
        hot = as_bf16(columns == index[:, pl.ds(pl.multiple_of(begin, size), size)])
        picked = sum(dot_nn(part, hot) for part in reversed(split3(image[...])))
        weight = dot_nn(spread(mask[...].astype(F32), 16).astype(jnp.bfloat16), hot)
        over = jnp.zeros((1, 1), F32)
    out[...] = picked
    weights[...] = weight
    count = jnp.sum(weight[0:1], axis=1, keepdims=True)
    line = lax.broadcasted_iota(jnp.int32, (8, 128), 0)
    info[...] = jnp.where(line == 0, count, over)


def select(compact, flip, place, image, index, mask):
    frames, band = image.shape
    size = ROOM if compact else index.shape[1] // 2
    return pl.pallas_call(
        functools.partial(select_kernel, compact, flip),
        out_shape=(
            jax.ShapeDtypeStruct((frames, size), F32),
            jax.ShapeDtypeStruct((16, size), F32),
            jax.ShapeDtypeStruct((8, 128), F32),
        ),
        in_specs=[SMEM, VMEM, VMEM, VMEM],
        out_specs=(VMEM, VMEM, VMEM),
        compiler_params=PARAMS,
        cost_estimate=pl.CostEstimate(
            flops=2 * frames * band * size * 3, bytes_accessed=frames * band * 4, transcendentals=0
        ),
        name="select",
    )(place, image, index, mask)


def gram_kernel(slots, last, place, info, weights, stay0, move0, *refs):
    backs, refs = (refs[:2], refs[2:]) if last else (refs[:4], refs[4:])
    previous, refs = refs[: -2 - len(slots)], refs[-2 - len(slots) :]
    outs, ordered, rows = refs[: len(slots)], refs[-2], refs[-1]
    zh, y, core, x, r = (place[i] for i in (0, 1, 2, 4, 5))
    frames, width = move0.shape
    owners = AXES["x"] * AXES["r"]
    mine = 2 * ROWS
    share_of = owners * mine
    size = len(slots) * share_of
    line = lax.broadcasted_iota(jnp.int32, (16, frames), 0)

    def terms(value):
        high, low = split2(value)
        return jnp.concatenate([high, low, high], axis=1)

    def blocks(pair):
        return [terms(block[...]) for block in pair]

    def place_of(owner, slot):
        apart = x ^ (owner // AXES["r"])
        near = 2 - (core ^ slot)
        chunk = jnp.where(apart == 3, 3 - near, jnp.where(apart == 1, near, apart + (apart >> 1)))
        return chunk, (owner % AXES["r"] - r) & 3

    for kind, left in enumerate((stay0[...], move0[...])):
        for at, slot in enumerate(slots):
            first = (core ^ slot) == 0
            for owner in range(owners):
                for l2 in range(2):
                    begin = owner // 4 * (frames // 4) + (l2 * 4 + owner % 4) * mine
                    to = at * share_of + owner * mine + l2 * ROWS
                    ordered[to : to + ROWS, :] = jnp.where(
                        first, left[begin : begin + ROWS], left[begin + ROWS : begin + mine]
                    )
        for begin, value in ((0, ordered[...] * weights[0:1]), (size, weights[...])):
            high, low = split2(value)
            rows[kind, begin : begin + value.shape[0], :] = jnp.concatenate(
                [high, high, low], axis=1
            )
    sums = jnp.where((line & 7) == SHIFTS, info[0:1, 0:1], 0.0)
    sums = jnp.where((line & 7) == SHIFTS + 1, info[1:2, 0:1], sums)
    if last:
        for out, before in zip(outs, previous):
            out[...] = before[...]
    if last:
        others = [(2, blocks(backs))]
    else:
        here = blocks((stay0, move0))
        others = [(0, here), (4, here)]
        others += [(1 + 2 * core, backs[:2]), (3 - 2 * core, backs[2:])]
    for shift, right in others:
        if isinstance(shift, int):
            flip = 1 if shift == 4 else (y < shift).astype(jnp.int32)
            begin_row = shift * 24
        else:
            flip, right = (y < shift).astype(jnp.int32), blocks(right)
            begin_row = pl.multiple_of(shift * 24, 8)
        stay, move = (dot_nt(rows[kind ^ flip], right[kind]) for kind in range(2))
        swap = (zh ^ flip) == 1
        tiles = jnp.where(swap, move, stay), jnp.where(swap, stay, move)
        for label in range(2):
            sums = jnp.where(line == label * 8 + shift, tiles[label][size : size + 1], sums)
        for at, out in enumerate(outs):
            for owner in range(owners):
                begin = at * share_of + owner * mine
                out[(*place_of(owner, slots[at]), pl.ds(begin_row, 24))] = jnp.concatenate(
                    [tile[begin : begin + mine] for tile in tiles], axis=0
                )
    for slot, out in zip(slots, outs):
        for owner in range(owners):
            where = (*place_of(owner, slot), slice(120, 136))
            out[where] = jnp.where((line & 7) == 2, sums, out[where]) if last else sums


def gram(slots, last, place, info, weights, stay0, move0, backs, previous=()):
    frames, width = move0.shape
    operands = [place, info, weights, stay0, move0, *backs, *previous]
    result = jax.ShapeDtypeStruct((AXES["x"], AXES["r"], 136, frames), F32)
    lines = len(slots) * frames // 2
    return pl.pallas_call(
        functools.partial(gram_kernel, slots, last),
        out_shape=(result,) * len(slots),
        in_specs=[SMEM] + [VMEM] * (len(operands) - 1),
        out_specs=(VMEM,) * len(slots),
        scratch_shapes=[
            pltpu.VMEM((lines, width), F32),
            pltpu.VMEM((2, lines + 16, 3 * width), jnp.bfloat16),
        ],
        compiler_params=PARAMS,
        cost_estimate=pl.CostEstimate(
            flops=len(slots) * (1 if last else 4) * 2 * frames * frames * width * 3,
            bytes_accessed=6 * frames * width * 4 + len(slots) * 5 * frames * frames * 4,
            transcendentals=0,
        ),
        name="gram",
    )(*operands)


def share_kernel(place, near, below, above, two, *outs):
    total = (near[0] + below[...]) + (above[...] + two[...])
    out = outs[-1]
    for zh in range(2):
        for l2 in range(2):
            to = (zh ^ place[0]) * 2 + (l2 ^ place[6])
            for shift in range(SHIFTS):
                begin = shift * 24 + zh * 12 + l2 * ROWS
                out[to, shift * ROWS : (shift + 1) * ROWS] = total[begin : begin + ROWS]
            out[to, 30:32] = jnp.zeros((2, total.shape[1]), F32)
            out[to, 32:40] = total[120 + zh * 8 : 128 + zh * 8]
    for to in range(4):
        outs[to][...] = out[to]


def share(place, *parts):
    frames = parts[-1].shape[-1]
    return pl.pallas_call(
        share_kernel,
        out_shape=(jax.ShapeDtypeStruct((40, frames), F32),) * 4,
        in_specs=[SMEM] + [VMEM] * 4,
        out_specs=(VMEM,) * 4,
        scratch_shapes=[pltpu.VMEM((4, 40, frames), F32)],
        compiler_params=PARAMS,
        name="share",
    )(place, *parts)


def finish_kernel(place, one, two, three, four, out, missing):
    total = (one[...] + two[...]) + (three[...] + four[...])
    frames = total.shape[1]
    sums = total[32 : 32 + SHIFTS]
    good = total[32 + SHIFTS : 33 + SHIFTS]
    line = lax.broadcasted_iota(jnp.int32, (ROWS, frames), 0)
    lane = lax.broadcasted_iota(jnp.int32, (ROWS, frames), 1)
    mine = jnp.where(lane == line + place[3], sums[0:1], 0.0)
    own = jnp.sum(mine, axis=1, keepdims=True)
    for shift in range(SHIFTS):
        tile = total[shift * ROWS : (shift + 1) * ROWS]
        out[shift] = tile * good / (own * sums[shift : shift + 1])
    missing[...] = jnp.broadcast_to(total[33 + SHIFTS : 34 + SHIFTS, :128], (8, 128))


def finish(place, *parts):
    return pl.pallas_call(
        finish_kernel,
        out_shape=(
            jax.ShapeDtypeStruct((SHIFTS, ROWS, parts[0].shape[-1]), F32),
            jax.ShapeDtypeStruct((8, 128), F32),
        ),
        in_specs=[SMEM] + [VMEM] * 4,
        out_specs=(VMEM, VMEM),
        compiler_params=PARAMS,
        name="finish",
    )(place, *parts)


def correlate(compact, place, intensity, index, mask):
    def after(value, *others):
        return lax.optimization_barrier((value, *others))[0]

    def first(value):
        return send(value, y=lambda at: at["y"] + 1 - 2 * at["core"])

    def second(value):
        return send(value, y=lambda at: at["y"] - 1 + 2 * at["core"])

    given, *_ = select(compact, 0, place, intensity, index, mask)
    moved = send(given, zh=lambda at: at["zh"] + 1)
    kept, weights, info = select(compact, 1, place, intensity, after(index, given), mask)
    kept_backs = first(kept), second(kept), send(kept, y=lambda at: at["y"] + 2)
    moved = after(jnp.where(weights[0:1] > 0, moved, 0.0), *kept_backs)
    moved_first, moved_second = first(moved), second(moved)
    moved_opposite = first(moved_first)
    blocks = (place, info, weights, kept, moved)
    backs = (kept_backs[0], moved_first, kept_backs[1], moved_second)
    early = gram((1, 0), False, *blocks, backs)
    backs = (kept_backs[2], moved_opposite)
    (give,) = gram((1,), True, *blocks, backs, early[:1])
    (keep,) = gram((0,), True, *blocks, backs, early[1:])

    total = keep + send(give, core=lambda at: 1 - at["core"])
    near = total[:2] + send(
        total[2:], x=lambda at: 3 - at["x"] if at["core"] else at["x"] ^ 1
    )
    near = near[0] + send(near[1], x=lambda at: at["x"] ^ 1 if at["core"] else 3 - at["x"])
    below = send(near[1], **along_z(1))
    above = send(near[3], **along_z(-1))
    middle = send(near[2], **along_z(lambda core: 2 - 4 * core))
    pieces = share(place, near, below, above, middle)
    far = send(pieces[2], zh=lambda at: at["zh"] + 1)
    farther = send(pieces[3], zh=lambda at: at["zh"] + 1, l2=lambda at: at["l2"] + 1)
    next_one = send(pieces[1], l2=lambda at: at["l2"] + 1)
    return finish(place, pieces[0], far, farther, next_one)


def body(intensity, circle_index, pixel_mask):
    place = jnp.stack(
        [
            lax.axis_index("zh"),
            lax.axis_index("y"),
            lax.axis_index("core"),
            lax.axis_index(PIX) * ROWS,
            lax.axis_index("x"),
            lax.axis_index("r"),
            lax.axis_index("l2"),
        ]
    ).astype(jnp.int32)
    operands = (place, intensity, circle_index[None, :], pixel_mask[None, :])
    result, missing = correlate(True, *operands)
    return lax.cond(
        missing[0, 0] > 0.5,
        lambda result, *operands: correlate(False, *operands)[0],
        lambda result, *operands: result,
        result,
        *operands,
    )


def solution(mesh):
    split = jax.sharding.Mesh(mesh.devices.reshape(tuple(AXES.values())), tuple(AXES))
    return jax.shard_map(
        body,
        mesh=split,
        in_specs=(P(FRAMES, PIX), P(PIX), P(PIX)),
        out_specs=P(None, (*FRAMES, *PIX), None),
        check_vma=False,
    )
```

```python
import functools
import math

import jax
import jax.numpy as jnp
import numpy as np
from jax import lax
from jax.experimental import pallas as pl
from jax.experimental.pallas import tpu as pltpu
from jax.sharding import PartitionSpec as P

AXES = {"zh": 2, "y": 4, "x": 4, "l2": 2, "r": 4, "core": 2}
FRAMES, PIX = ("zh", "y"), ("x", "l2", "r", "core")
SHIFTS = 5
ROWS = 6
ROOM = 384
VMEM = pl.BlockSpec(memory_space=pltpu.VMEM)
SMEM = pl.BlockSpec(memory_space=pltpu.SMEM)
PARAMS = pltpu.CompilerParams(vmem_limit_bytes=24 * 1024 * 1024)
F32 = jnp.float32


def send(value, **moves):
    names = tuple(AXES)
    sizes = tuple(AXES.values())
    pairs = []
    for source in range(math.prod(sizes)):
        at = dict(zip(names, (int(i) for i in np.unravel_index(source, sizes))))
        to = [moves[name](at) % AXES[name] if name in moves else at[name] for name in names]
        pairs.append((source, int(np.ravel_multi_index(to, sizes))))
    return lax.ppermute(value, names, pairs)


def along_z(by):
    def target(at):
        z = at["zh"] * 8 + at["l2"] * 4 + at["r"]
        return (z + (by(at["core"]) if callable(by) else by)) % 16

    return {
        "zh": lambda at: target(at) // 8,
        "l2": lambda at: target(at) // 4,
        "r": lambda at: target(at),
    }


def split2(value):
    high = value.astype(jnp.bfloat16)
    return high, (value - high.astype(F32)).astype(jnp.bfloat16)


def split3(value):
    high = value.astype(jnp.bfloat16)
    return (high, *split2(value - high.astype(F32)))


def as_bf16(value):
    return value.astype(F32).astype(jnp.bfloat16)


def spread(row, lines):
    return jnp.broadcast_to(row, (lines, row.shape[1]))


def dot_nn(left, right):
    return jnp.dot(left, right, preferred_element_type=F32)


def dot_nt(left, right):
    return lax.dot_general(left, right, (((1,), (1,)), ((), ())), preferred_element_type=F32)


def chosen(index, mask, begin, size):
    lanes = 128
    groups = mask.shape[1] // lanes
    padded = -(-groups // 16) * 16
    upper = lax.broadcasted_iota(jnp.int32, (padded, index.shape[1]), 0) == (index >> 7)
    lower = lax.broadcasted_iota(jnp.int32, (lanes, index.shape[1]), 0) == (index & (lanes - 1))
    times = dot_nt(as_bf16(upper), as_bf16(lower))
    rows = [mask[:, i * lanes : (i + 1) * lanes] for i in range(groups)]
    rows.append(jnp.zeros((padded - groups, lanes), jnp.int32))
    times = times * jnp.concatenate(rows, axis=0).astype(F32)
    used = as_bf16(times > 0)
    ahead = lax.broadcasted_iota(jnp.int32, (lanes, lanes), 0) < lax.broadcasted_iota(
        jnp.int32, (lanes, lanes), 1
    )
    above = lax.broadcasted_iota(jnp.int32, (padded, padded), 1) < lax.broadcasted_iota(
        jnp.int32, (padded, padded), 0
    )
    before = jnp.sum(dot_nn(as_bf16(above), used), axis=1, keepdims=True)
    number = dot_nn(used, as_bf16(ahead)) + before
    number = jnp.where(times > 0, number, -1.0).astype(jnp.int32)

    def in_line(value):
        return jnp.concatenate([value[i : i + 1] for i in range(groups)], axis=1)

    wanted = lax.broadcasted_iota(jnp.int32, (size, mask.shape[1]), 0) + begin
    total = jnp.sum(jnp.sum(used.astype(F32), axis=1, keepdims=True), axis=0, keepdims=True)
    return as_bf16(wanted == in_line(number)), in_line(times), total


def select_kernel(compact, flip, place, image, index, mask, out, weights, info):
    band = image.shape[1]
    size = out.shape[1]
    begin = (place[0] ^ flip) * size
    if compact:
        hot, times, total = chosen(index[...], mask[...], begin, size)
        picked = sum(dot_nt(part, hot) for part in reversed(split3(image[...])))
        weight = sum(dot_nt(part, hot) for part in reversed(split2(spread(times, 16))))
        over = jnp.where(total > 2.0 * size, 1.0, 0.0)
    else:
        columns = lax.broadcasted_iota(jnp.int32, (band, size), 0)
        hot = as_bf16(columns == index[:, pl.ds(pl.multiple_of(begin, size), size)])
        picked = sum(dot_nn(part, hot) for part in reversed(split3(image[...])))
        weight = dot_nn(spread(mask[...].astype(F32), 16).astype(jnp.bfloat16), hot)
        over = jnp.zeros((1, 1), F32)
    out[...] = picked
    weights[...] = weight
    count = jnp.sum(weight[0:1], axis=1, keepdims=True)
    line = lax.broadcasted_iota(jnp.int32, (8, 128), 0)
    info[...] = jnp.where(line == 0, count, over)


def select(compact, flip, place, image, index, mask):
    frames, band = image.shape
    size = ROOM if compact else index.shape[1] // 2
    return pl.pallas_call(
        functools.partial(select_kernel, compact, flip),
        out_shape=(
            jax.ShapeDtypeStruct((frames, size), F32),
            jax.ShapeDtypeStruct((16, size), F32),
            jax.ShapeDtypeStruct((8, 128), F32),
        ),
        in_specs=[SMEM, VMEM, VMEM, VMEM],
        out_specs=(VMEM, VMEM, VMEM),
        compiler_params=PARAMS,
        cost_estimate=pl.CostEstimate(
            flops=2 * frames * band * size * 3, bytes_accessed=frames * band * 4, transcendentals=0
        ),
        name="select",
    )(place, image, index, mask)


def gram_kernel(slots, last, place, info, weights, stay0, move0, *refs):
    backs, refs = (refs[:2], refs[2:]) if last else (refs[:4], refs[4:])
    previous, refs = refs[: -2 - len(slots)], refs[-2 - len(slots) :]
    outs, ordered, rows = refs[: len(slots)], refs[-2], refs[-1]
    zh, y, core, x, r = (place[i] for i in (0, 1, 2, 4, 5))
    frames, width = move0.shape
    owners = AXES["x"] * AXES["r"]
    mine = 2 * ROWS
    share_of = owners * mine
    size = len(slots) * share_of
    line = lax.broadcasted_iota(jnp.int32, (16, frames), 0)

    def terms(value):
        high, low = split2(value)
        return jnp.concatenate([high, low, high], axis=1)

    def blocks(pair):
        return [terms(block[...]) for block in pair]

    def place_of(owner, slot):
        apart = x ^ (owner // AXES["r"])
        near = 2 - (core ^ slot)
        chunk = jnp.where(apart == 3, 3 - near, jnp.where(apart == 1, near, apart + (apart >> 1)))
        return chunk, (owner % AXES["r"] - r) & 3

    for kind, left in enumerate((stay0[...], move0[...])):
        for at, slot in enumerate(slots):
            first = (core ^ slot) == 0
            for owner in range(owners):
                for l2 in range(2):
                    begin = owner // 4 * (frames // 4) + (l2 * 4 + owner % 4) * mine
                    to = at * share_of + owner * mine + l2 * ROWS
                    ordered[to : to + ROWS, :] = jnp.where(
                        first, left[begin : begin + ROWS], left[begin + ROWS : begin + mine]
                    )
        for begin, value in ((0, ordered[...] * weights[0:1]), (size, weights[...])):
            high, low = split2(value)
            rows[kind, begin : begin + value.shape[0], :] = jnp.concatenate(
                [high, high, low], axis=1
            )
    sums = jnp.where((line & 7) == SHIFTS, info[0:1, 0:1], 0.0)
    sums = jnp.where((line & 7) == SHIFTS + 1, info[1:2, 0:1], sums)
    if last:
        for out, before in zip(outs, previous):
            out[...] = before[...]
    if last:
        others = [(2, blocks(backs))]
    else:
        here = blocks((stay0, move0))
        others = [(0, here), (4, here)]
        others += [(1 + 2 * core, backs[:2]), (3 - 2 * core, backs[2:])]
    for shift, right in others:
        if isinstance(shift, int):
            flip = 1 if shift == 4 else (y < shift).astype(jnp.int32)
            begin_row = shift * 24
        else:
            flip, right = (y < shift).astype(jnp.int32), blocks(right)
            begin_row = pl.multiple_of(shift * 24, 8)
        stay, move = (dot_nt(rows[kind ^ flip], right[kind]) for kind in range(2))
        swap = (zh ^ flip) == 1
        tiles = jnp.where(swap, move, stay), jnp.where(swap, stay, move)
        for label in range(2):
            sums = jnp.where(line == label * 8 + shift, tiles[label][size : size + 1], sums)
        for at, out in enumerate(outs):
            for owner in range(owners):
                begin = at * share_of + owner * mine
                out[(*place_of(owner, slots[at]), pl.ds(begin_row, 24))] = jnp.concatenate(
                    [tile[begin : begin + mine] for tile in tiles], axis=0
                )
    for slot, out in zip(slots, outs):
        for owner in range(owners):
            where = (*place_of(owner, slot), slice(120, 136))
            out[where] = jnp.where((line & 7) == 2, sums, out[where]) if last else sums


def gram(slots, last, place, info, weights, stay0, move0, backs, previous=()):
    frames, width = move0.shape
    operands = [place, info, weights, stay0, move0, *backs, *previous]
    result = jax.ShapeDtypeStruct((AXES["x"], AXES["r"], 136, frames), F32)
    lines = len(slots) * frames // 2
    return pl.pallas_call(
        functools.partial(gram_kernel, slots, last),
        out_shape=(result,) * len(slots),
        in_specs=[SMEM] + [VMEM] * (len(operands) - 1),
        out_specs=(VMEM,) * len(slots),
        scratch_shapes=[
            pltpu.VMEM((lines, width), F32),
            pltpu.VMEM((2, lines + 16, 3 * width), jnp.bfloat16),
        ],
        compiler_params=PARAMS,
        cost_estimate=pl.CostEstimate(
            flops=len(slots) * (1 if last else 4) * 2 * frames * frames * width * 3,
            bytes_accessed=6 * frames * width * 4 + len(slots) * 5 * frames * frames * 4,
            transcendentals=0,
        ),
        name="gram",
    )(*operands)


def share_kernel(place, near, below, above, two, *outs):
    total = (near[0] + below[...]) + (above[...] + two[...])
    out = outs[-1]
    for zh in range(2):
        for l2 in range(2):
            to = (zh ^ place[0]) * 2 + (l2 ^ place[6])
            for shift in range(SHIFTS):
                begin = shift * 24 + zh * 12 + l2 * ROWS
                out[to, shift * ROWS : (shift + 1) * ROWS] = total[begin : begin + ROWS]
            out[to, 30:32] = jnp.zeros((2, total.shape[1]), F32)
            out[to, 32:40] = total[120 + zh * 8 : 128 + zh * 8]
    for to in range(4):
        outs[to][...] = out[to]


def share(place, *parts):
    frames = parts[-1].shape[-1]
    return pl.pallas_call(
        share_kernel,
        out_shape=(jax.ShapeDtypeStruct((40, frames), F32),) * 4,
        in_specs=[SMEM] + [VMEM] * 4,
        out_specs=(VMEM,) * 4,
        scratch_shapes=[pltpu.VMEM((4, 40, frames), F32)],
        compiler_params=PARAMS,
        name="share",
    )(place, *parts)


def finish_kernel(place, one, two, three, four, out, missing):
    total = (one[...] + two[...]) + (three[...] + four[...])
    frames = total.shape[1]
    sums = total[32 : 32 + SHIFTS]
    good = total[32 + SHIFTS : 33 + SHIFTS]
    line = lax.broadcasted_iota(jnp.int32, (ROWS, frames), 0)
    lane = lax.broadcasted_iota(jnp.int32, (ROWS, frames), 1)
    mine = jnp.where(lane == line + place[3], sums[0:1], 0.0)
    own = jnp.sum(mine, axis=1, keepdims=True)
    for shift in range(SHIFTS):
        tile = total[shift * ROWS : (shift + 1) * ROWS]
        out[shift] = tile * good / (own * sums[shift : shift + 1])
    missing[...] = jnp.broadcast_to(total[33 + SHIFTS : 34 + SHIFTS, :128], (8, 128))


def finish(place, *parts):
    return pl.pallas_call(
        finish_kernel,
        out_shape=(
            jax.ShapeDtypeStruct((SHIFTS, ROWS, parts[0].shape[-1]), F32),
            jax.ShapeDtypeStruct((8, 128), F32),
        ),
        in_specs=[SMEM] + [VMEM] * 4,
        out_specs=(VMEM, VMEM),
        compiler_params=PARAMS,
        name="finish",
    )(place, *parts)


def correlate(compact, place, intensity, index, mask):
    def after(value, *others):
        return lax.optimization_barrier((value, *others))[0]

    def first(value):
        return send(value, y=lambda at: at["y"] + 1 - 2 * at["core"])

    def second(value):
        return send(value, y=lambda at: at["y"] - 1 + 2 * at["core"])

    given, *_ = select(compact, 0, place, intensity, index, mask)
    moved = send(given, zh=lambda at: at["zh"] + 1)
    kept, weights, info = select(compact, 1, place, intensity, after(index, given), mask)
    kept_backs = first(kept), second(kept), send(kept, y=lambda at: at["y"] + 2)
    moved = after(jnp.where(weights[0:1] > 0, moved, 0.0), *kept_backs)
    moved_first, moved_second = first(moved), second(moved)
    moved_opposite = first(moved_first)
    blocks = (place, info, weights, kept, moved)
    backs = (kept_backs[0], moved_first, kept_backs[1], moved_second)
    early = gram((1, 0), False, *blocks, backs)
    backs = (kept_backs[2], moved_opposite)
    (give,) = gram((1,), True, *blocks, backs, early[:1])
    (keep,) = gram((0,), True, *blocks, backs, early[1:])

    away = keep[2:] + send(give[2:], core=lambda at: 1 - at["core"])
    near = keep[:2] + send(give[:2], core=lambda at: 1 - at["core"])
    near = near + send(away, x=lambda at: 3 - at["x"] if at["core"] else at["x"] ^ 1)
    near = near[0] + send(near[1], x=lambda at: at["x"] ^ 1 if at["core"] else 3 - at["x"])
    below = send(near[1], **along_z(1))
    above = send(near[3], **along_z(-1))
    middle = send(near[2], **along_z(lambda core: 2 - 4 * core))
    pieces = share(place, near, below, above, middle)
    far = send(pieces[2], zh=lambda at: at["zh"] + 1)
    farther = send(pieces[3], zh=lambda at: at["zh"] + 1, l2=lambda at: at["l2"] + 1)
    next_one = send(pieces[1], l2=lambda at: at["l2"] + 1)
    return finish(place, pieces[0], far, farther, next_one)


def body(intensity, circle_index, pixel_mask):
    place = jnp.stack(
        [
            lax.axis_index("zh"),
            lax.axis_index("y"),
            lax.axis_index("core"),
            lax.axis_index(PIX) * ROWS,
            lax.axis_index("x"),
            lax.axis_index("r"),
            lax.axis_index("l2"),
        ]
    ).astype(jnp.int32)
    operands = (place, intensity, circle_index[None, :], pixel_mask[None, :])
    result, missing = correlate(True, *operands)
    return lax.cond(
        missing[0, 0] > 0.5,
        lambda result, *operands: correlate(False, *operands)[0],
        lambda result, *operands: result,
        result,
        *operands,
    )


def solution(mesh):
    split = jax.sharding.Mesh(mesh.devices.reshape(tuple(AXES.values())), tuple(AXES))
    return jax.shard_map(
        body,
        mesh=split,
        in_specs=(P(FRAMES, PIX), P(PIX), P(PIX)),
        out_specs=P(None, (*FRAMES, *PIX), None),
        check_vma=False,
    )
```

```python
import functools
import math

import jax
import jax.numpy as jnp
import numpy as np
from jax import lax
from jax.experimental import pallas as pl
from jax.experimental.pallas import tpu as pltpu
from jax.sharding import PartitionSpec as P

AXES = {"zh": 2, "y": 4, "x": 4, "l2": 2, "r": 4, "core": 2}
FRAMES, PIX = ("zh", "y"), ("x", "l2", "r", "core")
SHIFTS = 5
ROWS = 6
ROOM = 384
VMEM = pl.BlockSpec(memory_space=pltpu.VMEM)
SMEM = pl.BlockSpec(memory_space=pltpu.SMEM)
PARAMS = pltpu.CompilerParams(vmem_limit_bytes=24 * 1024 * 1024)
F32 = jnp.float32


def send(value, **moves):
    names = tuple(AXES)
    sizes = tuple(AXES.values())
    pairs = []
    for source in range(math.prod(sizes)):
        at = dict(zip(names, (int(i) for i in np.unravel_index(source, sizes))))
        to = [moves[name](at) % AXES[name] if name in moves else at[name] for name in names]
        pairs.append((source, int(np.ravel_multi_index(to, sizes))))
    return lax.ppermute(value, names, pairs)


def along_z(by):
    def target(at):
        z = at["zh"] * 8 + at["l2"] * 4 + at["r"]
        return (z + (by(at["core"]) if callable(by) else by)) % 16

    return {
        "zh": lambda at: target(at) // 8,
        "l2": lambda at: target(at) // 4,
        "r": lambda at: target(at),
    }


def split2(value):
    high = value.astype(jnp.bfloat16)
    return high, (value - high.astype(F32)).astype(jnp.bfloat16)


def split3(value):
    high = value.astype(jnp.bfloat16)
    return (high, *split2(value - high.astype(F32)))


def as_bf16(value):
    return value.astype(F32).astype(jnp.bfloat16)


def spread(row, lines):
    return jnp.broadcast_to(row, (lines, row.shape[1]))


def dot_nn(left, right):
    return jnp.dot(left, right, preferred_element_type=F32)


def dot_nt(left, right):
    return lax.dot_general(left, right, (((1,), (1,)), ((), ())), preferred_element_type=F32)


def chosen(index, mask, begin, size):
    lanes = 128
    groups = mask.shape[1] // lanes
    padded = -(-groups // 16) * 16
    upper = lax.broadcasted_iota(jnp.int32, (padded, index.shape[1]), 0) == (index >> 7)
    lower = lax.broadcasted_iota(jnp.int32, (lanes, index.shape[1]), 0) == (index & (lanes - 1))
    times = dot_nt(as_bf16(upper), as_bf16(lower))
    rows = [mask[:, i * lanes : (i + 1) * lanes] for i in range(groups)]
    rows.append(jnp.zeros((padded - groups, lanes), jnp.int32))
    times = times * jnp.concatenate(rows, axis=0).astype(F32)
    used = as_bf16(times > 0)
    ahead = lax.broadcasted_iota(jnp.int32, (lanes, lanes), 0) < lax.broadcasted_iota(
        jnp.int32, (lanes, lanes), 1
    )
    above = lax.broadcasted_iota(jnp.int32, (padded, padded), 1) < lax.broadcasted_iota(
        jnp.int32, (padded, padded), 0
    )
    before = jnp.sum(dot_nn(as_bf16(above), used), axis=1, keepdims=True)
    number = dot_nn(used, as_bf16(ahead)) + before
    number = jnp.where(times > 0, number, -1.0).astype(jnp.int32)

    def in_line(value):
        return jnp.concatenate([value[i : i + 1] for i in range(groups)], axis=1)

    wanted = lax.broadcasted_iota(jnp.int32, (size, mask.shape[1]), 0) + begin
    total = jnp.sum(jnp.sum(used.astype(F32), axis=1, keepdims=True), axis=0, keepdims=True)
    return as_bf16(wanted == in_line(number)), in_line(times), total


def select_kernel(compact, flip, place, image, index, mask, out, weights, info):
    band = image.shape[1]
    size = out.shape[1]
    begin = (place[0] ^ flip) * size
    if compact:
        hot, times, total = chosen(index[...], mask[...], begin, size)
        picked = sum(dot_nt(part, hot) for part in reversed(split2(image[...])))
        weight = sum(dot_nt(part, hot) for part in reversed(split2(spread(times, 16))))
        over = jnp.where(total > 2.0 * size, 1.0, 0.0)
    else:
        columns = lax.broadcasted_iota(jnp.int32, (band, size), 0)
        hot = as_bf16(columns == index[:, pl.ds(pl.multiple_of(begin, size), size)])
        picked = sum(dot_nn(part, hot) for part in reversed(split2(image[...])))
        weight = dot_nn(spread(mask[...].astype(F32), 16).astype(jnp.bfloat16), hot)
        over = jnp.zeros((1, 1), F32)
    out[...] = picked
    weights[...] = weight
    count = jnp.sum(weight[0:1], axis=1, keepdims=True)
    line = lax.broadcasted_iota(jnp.int32, (8, 128), 0)
    info[...] = jnp.where(line == 0, count, over)


def select(compact, flip, place, image, index, mask):
    frames, band = image.shape
    size = ROOM if compact else index.shape[1] // 2
    return pl.pallas_call(
        functools.partial(select_kernel, compact, flip),
        out_shape=(
            jax.ShapeDtypeStruct((frames, size), F32),
            jax.ShapeDtypeStruct((16, size), F32),
            jax.ShapeDtypeStruct((8, 128), F32),
        ),
        in_specs=[SMEM, VMEM, VMEM, VMEM],
        out_specs=(VMEM, VMEM, VMEM),
        compiler_params=PARAMS,
        cost_estimate=pl.CostEstimate(
            flops=2 * frames * band * size * 3, bytes_accessed=frames * band * 4, transcendentals=0
        ),
        name="select",
    )(place, image, index, mask)


def gram_kernel(slots, last, place, info, weights, stay0, move0, *refs):
    backs, refs = (refs[:2], refs[2:]) if last else (refs[:4], refs[4:])
    previous, refs = refs[: -2 - len(slots)], refs[-2 - len(slots) :]
    outs, ordered, rows = refs[: len(slots)], refs[-2], refs[-1]
    zh, y, core, x, r = (place[i] for i in (0, 1, 2, 4, 5))
    frames, width = move0.shape
    owners = AXES["x"] * AXES["r"]
    mine = 2 * ROWS
    share_of = owners * mine
    size = len(slots) * share_of
    line = lax.broadcasted_iota(jnp.int32, (16, frames), 0)

    def terms(value):
        high, low = split2(value)
        return jnp.concatenate([high, low, high], axis=1)

    def blocks(pair):
        return [terms(block[...]) for block in pair]

    def place_of(owner, slot):
        apart = x ^ (owner // AXES["r"])
        near = 2 - (core ^ slot)
        chunk = jnp.where(apart == 3, 3 - near, jnp.where(apart == 1, near, apart + (apart >> 1)))
        return chunk, (owner % AXES["r"] - r) & 3

    for kind, left in enumerate((stay0[...], move0[...])):
        for at, slot in enumerate(slots):
            first = (core ^ slot) == 0
            for owner in range(owners):
                for l2 in range(2):
                    begin = owner // 4 * (frames // 4) + (l2 * 4 + owner % 4) * mine
                    to = at * share_of + owner * mine + l2 * ROWS
                    ordered[to : to + ROWS, :] = jnp.where(
                        first, left[begin : begin + ROWS], left[begin + ROWS : begin + mine]
                    )
        for begin, value in ((0, ordered[...] * weights[0:1]), (size, weights[...])):
            high, low = split2(value)
            rows[kind, begin : begin + value.shape[0], :] = jnp.concatenate(
                [high, high, low], axis=1
            )
    sums = jnp.where((line & 7) == SHIFTS, info[0:1, 0:1], 0.0)
    sums = jnp.where((line & 7) == SHIFTS + 1, info[1:2, 0:1], sums)
    if last:
        for out, before in zip(outs, previous):
            out[...] = before[...]
    if last:
        others = [(2, blocks(backs))]
    else:
        here = blocks((stay0, move0))
        others = [(0, here), (4, here)]
        others += [(1 + 2 * core, backs[:2]), (3 - 2 * core, backs[2:])]
    for shift, right in others:
        if isinstance(shift, int):
            flip = 1 if shift == 4 else (y < shift).astype(jnp.int32)
            begin_row = shift * 24
        else:
            flip, right = (y < shift).astype(jnp.int32), blocks(right)
            begin_row = pl.multiple_of(shift * 24, 8)
        stay, move = (dot_nt(rows[kind ^ flip], right[kind]) for kind in range(2))
        swap = (zh ^ flip) == 1
        tiles = jnp.where(swap, move, stay), jnp.where(swap, stay, move)
        for label in range(2):
            sums = jnp.where(line == label * 8 + shift, tiles[label][size : size + 1], sums)
        for at, out in enumerate(outs):
            for owner in range(owners):
                begin = at * share_of + owner * mine
                out[(*place_of(owner, slots[at]), pl.ds(begin_row, 24))] = jnp.concatenate(
                    [tile[begin : begin + mine] for tile in tiles], axis=0
                )
    for slot, out in zip(slots, outs):
        for owner in range(owners):
            where = (*place_of(owner, slot), slice(120, 136))
            out[where] = jnp.where((line & 7) == 2, sums, out[where]) if last else sums


def gram(slots, last, place, info, weights, stay0, move0, backs, previous=()):
    frames, width = move0.shape
    operands = [place, info, weights, stay0, move0, *backs, *previous]
    result = jax.ShapeDtypeStruct((AXES["x"], AXES["r"], 136, frames), F32)
    lines = len(slots) * frames // 2
    return pl.pallas_call(
        functools.partial(gram_kernel, slots, last),
        out_shape=(result,) * len(slots),
        in_specs=[SMEM] + [VMEM] * (len(operands) - 1),
        out_specs=(VMEM,) * len(slots),
        scratch_shapes=[
            pltpu.VMEM((lines, width), F32),
            pltpu.VMEM((2, lines + 16, 3 * width), jnp.bfloat16),
        ],
        compiler_params=PARAMS,
        cost_estimate=pl.CostEstimate(
            flops=len(slots) * (1 if last else 4) * 2 * frames * frames * width * 3,
            bytes_accessed=6 * frames * width * 4 + len(slots) * 5 * frames * frames * 4,
            transcendentals=0,
        ),
        name="gram",
    )(*operands)


def share_kernel(place, near, below, above, two, *outs):
    total = (near[0] + below[...]) + (above[...] + two[...])
    out = outs[-1]
    for zh in range(2):
        for l2 in range(2):
            to = (zh ^ place[0]) * 2 + (l2 ^ place[6])
            for shift in range(SHIFTS):
                begin = shift * 24 + zh * 12 + l2 * ROWS
                out[to, shift * ROWS : (shift + 1) * ROWS] = total[begin : begin + ROWS]
            out[to, 30:32] = jnp.zeros((2, total.shape[1]), F32)
            out[to, 32:40] = total[120 + zh * 8 : 128 + zh * 8]
    for to in range(4):
        outs[to][...] = out[to]


def share(place, *parts):
    frames = parts[-1].shape[-1]
    return pl.pallas_call(
        share_kernel,
        out_shape=(jax.ShapeDtypeStruct((40, frames), F32),) * 4,
        in_specs=[SMEM] + [VMEM] * 4,
        out_specs=(VMEM,) * 4,
        scratch_shapes=[pltpu.VMEM((4, 40, frames), F32)],
        compiler_params=PARAMS,
        name="share",
    )(place, *parts)


def finish_kernel(place, one, two, three, four, out, missing):
    total = (one[...] + two[...]) + (three[...] + four[...])
    frames = total.shape[1]
    sums = total[32 : 32 + SHIFTS]
    good = total[32 + SHIFTS : 33 + SHIFTS]
    line = lax.broadcasted_iota(jnp.int32, (ROWS, frames), 0)
    lane = lax.broadcasted_iota(jnp.int32, (ROWS, frames), 1)
    mine = jnp.where(lane == line + place[3], sums[0:1], 0.0)
    own = jnp.sum(mine, axis=1, keepdims=True)
    for shift in range(SHIFTS):
        tile = total[shift * ROWS : (shift + 1) * ROWS]
        out[shift] = tile * good / (own * sums[shift : shift + 1])
    missing[...] = jnp.broadcast_to(total[33 + SHIFTS : 34 + SHIFTS, :128], (8, 128))


def finish(place, *parts):
    return pl.pallas_call(
        finish_kernel,
        out_shape=(
            jax.ShapeDtypeStruct((SHIFTS, ROWS, parts[0].shape[-1]), F32),
            jax.ShapeDtypeStruct((8, 128), F32),
        ),
        in_specs=[SMEM] + [VMEM] * 4,
        out_specs=(VMEM, VMEM),
        compiler_params=PARAMS,
        name="finish",
    )(place, *parts)


def correlate(compact, place, intensity, index, mask):
    def after(value, *others):
        return lax.optimization_barrier((value, *others))[0]

    def first(value):
        return send(value, y=lambda at: at["y"] + 1 - 2 * at["core"])

    def second(value):
        return send(value, y=lambda at: at["y"] - 1 + 2 * at["core"])

    given, *_ = select(compact, 0, place, intensity, index, mask)
    moved = send(given, zh=lambda at: at["zh"] + 1)
    kept, weights, info = select(compact, 1, place, intensity, after(index, given), mask)
    kept_backs = first(kept), second(kept), send(kept, y=lambda at: at["y"] + 2)
    moved = after(jnp.where(weights[0:1] > 0, moved, 0.0), *kept_backs)
    moved_first, moved_second = first(moved), second(moved)
    moved_opposite = first(moved_first)
    blocks = (place, info, weights, kept, moved)
    backs = (kept_backs[0], moved_first, kept_backs[1], moved_second)
    early = gram((1, 0), False, *blocks, backs)
    backs = (kept_backs[2], moved_opposite)
    (give,) = gram((1,), True, *blocks, backs, early[:1])
    (keep,) = gram((0,), True, *blocks, backs, early[1:])

    away = keep[2:] + send(give[2:], core=lambda at: 1 - at["core"])
    near = keep[:2] + send(give[:2], core=lambda at: 1 - at["core"])
    near = near + send(away, x=lambda at: 3 - at["x"] if at["core"] else at["x"] ^ 1)
    near = near[0] + send(near[1], x=lambda at: at["x"] ^ 1 if at["core"] else 3 - at["x"])
    below = send(near[1], **along_z(1))
    above = send(near[3], **along_z(-1))
    middle = send(near[2], **along_z(lambda core: 2 - 4 * core))
    pieces = share(place, near, below, above, middle)
    far = send(pieces[2], zh=lambda at: at["zh"] + 1)
    farther = send(pieces[3], zh=lambda at: at["zh"] + 1, l2=lambda at: at["l2"] + 1)
    next_one = send(pieces[1], l2=lambda at: at["l2"] + 1)
    return finish(place, pieces[0], far, farther, next_one)


def body(intensity, circle_index, pixel_mask):
    place = jnp.stack(
        [
            lax.axis_index("zh"),
            lax.axis_index("y"),
            lax.axis_index("core"),
            lax.axis_index(PIX) * ROWS,
            lax.axis_index("x"),
            lax.axis_index("r"),
            lax.axis_index("l2"),
        ]
    ).astype(jnp.int32)
    operands = (place, intensity, circle_index[None, :], pixel_mask[None, :])
    result, missing = correlate(True, *operands)
    return lax.cond(
        missing[0, 0] > 0.5,
        lambda result, *operands: correlate(False, *operands)[0],
        lambda result, *operands: result,
        result,
        *operands,
    )


def solution(mesh):
    split = jax.sharding.Mesh(mesh.devices.reshape(tuple(AXES.values())), tuple(AXES))
    return jax.shard_map(
        body,
        mesh=split,
        in_specs=(P(FRAMES, PIX), P(PIX), P(PIX)),
        out_specs=P(None, (*FRAMES, *PIX), None),
        check_vma=False,
    )
```
